512 devices in a mesh: dom: 128 (over z, x, core), tile: 4 (over y).
Axes of the slice: x: 4, y: 4, z: 16, core: 2. Of those that a mesh axis runs over, the one named last changes fastest.
Arguments:
- vectors: float32 [4, 16, 131072], P(None, 'tile', 'dom'), may hold values from -6 to 6
- positions: float32 [3, 131072], P(None, 'dom'), may hold values from -8 to 8
- onsite: float32 [4, 131072], P(None, 'dom'), may hold values from -1.5 to 1.5
- neighbors: int32 [4, 131072], P(None, 'dom'), may hold values from 0 to 1280, as said below
Outputs:
- local_gamma: float32 [16, 131072], P('tile', 'dom')
The draws below stay inside these ranges and needn't reach their ends.
Inputs may be any that keep to these rules, and one draw needn't show every extreme that they name: `neighbors`: bonds are symmetric: if atom i names j then j names i. Codes below 128 appear only on a domain's first 128 slots and codes from 1152 to 1279 only on its last 128 slots (first column only); the number of bonds between two neighbouring domains varies from pair to pair, at most 128, reached by some pair. Slots of a domain that hold no atom have only the code 1024 + 2 * 128; the count of such slots varies between domains.
All inputs are finite; a program needn't handle non-finite values.
Results may differ from the reference program's by a relative error of at most 0.0002.
Values sent between devices are 32-bit elements; how exact they have to be, the bound alone decides.
A program may use at most 64 MiB of HBM per device.

```python
import jax
import jax.numpy as jnp
from jax import lax

A_DEV = 1024
BND = 128
VECS = 16
NORB = 4
NMOM = 4
ATOMS = 131072
N_DOM = 128


def draw_neighbors(key, part):
    ndom = ATOMS // A_DEV
    inner = A_DEV - 2 * BND
    none_index = A_DEV + 2 * BND
    key_count, key_fill, key_perm, key_match = jax.random.split(key, 4)
    bcount = jax.random.randint(key_count, (ndom,), BND // 2, BND + 1).at[0].set(BND)
    fill = jax.random.randint(key_fill, (ndom,), inner // 2, inner + 1).at[ndom - 1].set(inner)
    perms = jax.vmap(lambda sub: jax.random.permutation(sub, BND))(jax.random.split(key_perm, ndom)).astype(jnp.int32)
    inverse = jnp.argsort(perms, axis=1).astype(jnp.int32)
    prev_inverse = jnp.roll(inverse, 1, axis=0)
    prev_count = jnp.roll(bcount, 1)
    slots = jnp.arange(A_DEV, dtype=jnp.int32)

    def matching(sub, mask, count):
        perm = jax.random.permutation(sub, A_DEV).astype(jnp.int32)
        score = jnp.where(mask, perm, A_DEV + perm)
        order = jnp.argsort(score).astype(jnp.int32)
        rank = jnp.argsort(order).astype(jnp.int32)
        mate = jnp.bitwise_xor(rank, 1)
        partner = order[jnp.minimum(mate, A_DEV - 1)]
        valid = mask & (mate < count)
        return jnp.where(valid, partner + BND, none_index)

    def one_domain(sub, count_up, perm_up, count_down, inverse_down, filled):
        used = (slots < BND) | (slots >= A_DEV - BND) | (slots - BND < filled)
        inner_used = (slots >= BND) & (slots < A_DEV - BND) & (slots - BND < filled)
        keys = jax.random.split(sub, 4)
        ghost = inverse_down[jnp.minimum(slots, BND - 1)]
        lower = jnp.where(ghost < count_down, ghost, none_index)
        upper_slot = jnp.clip(slots - (A_DEV - BND), 0, BND - 1)
        upper = jnp.where(upper_slot < count_up, A_DEV + BND + perm_up[upper_slot], none_index)
        first = jnp.where(slots < BND, lower, jnp.where(slots >= A_DEV - BND, upper, matching(keys[0], inner_used, filled)))
        columns = [first]
        for column in range(1, 4):
            columns.append(matching(keys[column], used, 2 * BND + filled))
        return jnp.stack(columns)
    result = jax.vmap(one_domain)(jax.random.split(key_match, ndom), bcount, perms, prev_count, prev_inverse, fill)
    return jnp.transpose(result, (1, 0, 2)).reshape(4, ATOMS).astype(jnp.int32)


def block_levels(key, shape, cuts, smallest, high):
    gain, own = 1.0, jax.random.fold_in(key, 6)
    for axis_at, blocks in cuts:
        draws = jnp.exp(jax.random.uniform(jax.random.fold_in(own, axis_at), (blocks,), jnp.float32, smallest / len(cuts), high / len(cuts)))
        gain = gain * jnp.repeat(draws, shape[axis_at] // blocks).reshape([-1 if axis == axis_at else 1 for axis in range(len(shape))])
    return gain


def bell_draw(rng, shape, spread, bound, cuts=(), kind=jnp.bfloat16):
    values = spread * jax.random.normal(rng, shape, jnp.float32)
    if cuts:
        values = values * block_levels(rng, shape, cuts, -0.22, 0.18)
    return jnp.clip(values, -bound, bound).astype(kind)


def setup_inputs(seed: int = 0) -> dict:
    key_of = jax.random.split(jax.random.key(seed), 5)
    return {
        "vectors": bell_draw(key_of[0], (NORB, VECS, ATOMS), 1.0, 6.0, ((1, 4), (2, 128)), jnp.float32),
        "positions": bell_draw(key_of[1], (3, ATOMS), 1.4, 8.0, ((1, 128),), jnp.float32),
        "onsite": jnp.clip(jax.random.uniform(key_of[2], (NORB, ATOMS), jnp.float32, -1.5, 1.5) * block_levels(key_of[2], (NORB, ATOMS), ((1, 128),), -0.4, 0.0), -1.5, 1.5),
        "neighbors": draw_neighbors(jax.random.fold_in(key_of[4], 71), 0),
    }


onsite_s = -4.2
onsite_p = 1.72
hop_ss = -2.08
hop_sp = 2.48
hop_pps = 2.72
hop_ppp = -0.72
bond_length = 2.35
energy_scale = 16.0
length_scale = 2.0

def slater_koster(offset, bonded):
    distance = jnp.sqrt(lax.optimization_barrier(jnp.sum(offset * offset, axis=0)))
    radial = jnp.exp(-0.5 * (distance - bond_length) * (distance - bond_length)) * bonded / energy_scale
    cosines = offset / jnp.maximum(distance, 1.0)
    block_rows = [jnp.stack([jnp.full_like(radial, hop_ss), hop_sp * cosines[0], hop_sp * cosines[1], hop_sp * cosines[2]])]
    for row_axis in range(3):
        entries = [-hop_sp * cosines[row_axis]]
        for col_axis in range(3):
            extra = hop_ppp if row_axis == col_axis else 0.0
            entries.append(cosines[row_axis] * cosines[col_axis] * (hop_pps - hop_ppp) + extra)
        block_rows.append(jnp.stack(entries))
    return (jnp.stack(block_rows) * radial, -offset[0] / length_scale)

def reference(vectors, positions, onsite, neighbors):
    atoms = positions.shape[1]
    none_index = A_DEV + 2 * BND
    domain = jnp.arange(atoms, dtype=jnp.int32) // A_DEV
    below = (domain - 1) % N_DOM * A_DEV + A_DEV - BND + neighbors
    inside = domain * A_DEV + neighbors - BND
    above = (domain + 1) % N_DOM * A_DEV + neighbors - A_DEV - BND
    global_index = jnp.where(neighbors < BND, below, jnp.where(neighbors < A_DEV + BND, inside, jnp.where(neighbors < none_index, above, atoms))).astype(jnp.int32)
    padded_pos = jnp.concatenate([positions, jnp.zeros((3, 1), jnp.float32)], axis=1)
    blocks = []
    drifts = []
    for bond_index in range(4):
        offset = jnp.take(padded_pos, global_index[bond_index], axis=1) - positions
        bonded = (neighbors[bond_index] < none_index).astype(jnp.float32)
        block, drift = slater_koster(offset, bonded)
        blocks.append(block)
        drifts.append(drift)
    base = jnp.array([onsite_s, onsite_p, onsite_p, onsite_p], jnp.float32)
    diagonal = (base[:, None] + onsite) / energy_scale

    def apply_both(field, kcount):
        padded = jnp.concatenate([field, jnp.zeros((4, field.shape[1], 1), jnp.float32)], axis=2)
        hsum = jnp.zeros(field.shape, jnp.float32)
        ksum = jnp.zeros((4, kcount, atoms), jnp.float32)
        for bond_index in range(4):
            beside = jnp.take(padded, global_index[bond_index], axis=2)
            product = lax.optimization_barrier(jnp.sum(blocks[bond_index][:, :, None, :] * beside[None], axis=1))
            hsum = hsum + product
            ksum = ksum + drifts[bond_index] * product[:, :kcount]
        return (diagonal[:, None, :] * field + hsum, ksum)
    group = 4
    total = jnp.zeros((NMOM * NMOM, atoms), jnp.float32)
    for group_index in range(VECS // group):
        start_vec = vectors[:, group_index * group:(group_index + 1) * group, :]
        a_list = [start_vec]
        c_list = []
        hv, kv = apply_both(start_vec, group)
        a_list.append(hv)
        c_list.append(kv)
        for step in range(1, NMOM):
            hv, kv = apply_both(a_list[step], group)
            c_list.append(kv)
            if step + 1 < NMOM:
                a_list.append(2.0 * hv - a_list[step - 1])
        b_list = [c_list[0]]
        for step in range(NMOM - 1):
            hv, kv = apply_both(b_list[step], 0)
            if step == 0:
                b_list.append(hv)
            else:
                b_list.append(2.0 * hv - b_list[step - 1])
        b_stack = jnp.stack(b_list)
        c_stack = jnp.stack(c_list)
        terms = jnp.einsum('nopa,mopa->nma', b_stack, c_stack, precision=lax.Precision.HIGHEST)
        total = total + terms.reshape(NMOM * NMOM, atoms)
    return -total / VECS
```

```python
import jax
import jax.numpy as jnp
from jax import lax
from jax.experimental import pallas as pl
from jax.experimental.pallas import tpu as pltpu
from jax.sharding import PartitionSpec as P

BND = 128
VECS = 16
NMOM = 4
NORB = 4
LANES = 128
GROUPS = 8

onsite_s = -4.2
onsite_p = 1.72
hop_ss = -2.08
hop_sp = 2.48
hop_pps = 2.72
hop_ppp = -0.72
bond_length = 2.35
energy_scale = 16.0
length_scale = 2.0

MESH = pl.DeviceIdType.MESH
F32 = jnp.float32
TILE = (GROUPS, LANES)


def lanes_of(source, index):
    return jnp.take_along_axis(source, index, axis=1, mode="promise_in_bounds")


def pick(bits, options):
    for bit in bits:
        options = [jnp.where(bit, options[i + 1], options[i]) for i in range(0, len(options), 2)]
    return options[0]


def kernel(
    ndom, ntile,
    vec_hbm, pos_hbm, ons_hbm, nei_hbm, out_ref,
    vec_in, pos_in, ons_in, nei_in,
    pos, diag, code, low, geo, a_all, b_all, c_all, h_a, h_b, k_a,
    send0, send, ghost0, ghost, mom, mom_in,
    in_sem, halo_send, halo_recv, mom_send, mom_recv,
):
    dom, tile = lax.axis_index("dom"), lax.axis_index("tile")
    up, down = lax.rem(dom + 1, ndom), lax.rem(dom + ndom - 1, ndom)

    barrier = pltpu.get_barrier_semaphore()
    for other in (up, down):
        pl.semaphore_signal(barrier, inc=1, device_id={"dom": other}, device_id_type=MESH)
    for step in range(1, ntile):
        peer = lax.rem(tile + step, ntile)
        pl.semaphore_signal(barrier, inc=1, device_id={"tile": peer}, device_id_type=MESH)

    loads = [
        pltpu.make_async_copy(source, target, in_sem.at[i])
        for i, (source, target) in enumerate(
            ((vec_hbm, vec_in), (pos_hbm, pos_in), (nei_hbm, nei_in), (ons_hbm, ons_in))
        )
    ]
    for load in loads:
        load.start()
    for load in loads:
        load.wait()

    for group in range(GROUPS):
        cut = pl.ds(group * LANES, LANES)
        for orbital in range(NORB):
            a_all[0, pl.ds(orbital * 4, 4), group, :] = vec_in[orbital, :, cut]
        pos[:, group, :] = pos_in[:, cut]
        diag[:, group, :] = ons_in[:, cut]
        code[:, group, :] = nei_in[:, cut]
    for side, group in ((0, 0), (1, GROUPS - 1)):
        cut = pl.ds(group * LANES, LANES)
        for orbital in range(NORB):
            send0[side, pl.ds(orbital * 4, 4), :] = vec_in[orbital, :, cut]
        send0[side, pl.ds(16, 3), :] = pos_in[:, cut]

    def halo(step):
        copies = []
        for side, other in ((0, down), (1, up)):
            source, target = (send0.at[side], ghost0.at[1 - side]) if step == 0 else (
                send.at[step - 1, side], ghost.at[step - 1, 1 - side])
            copies.append(pltpu.make_async_remote_copy(
                src_ref=source, dst_ref=target,
                send_sem=halo_send.at[step, side], recv_sem=halo_recv.at[step, 1 - side],
                device_id={"dom": other}, device_id_type=MESH,
            ))
        return copies

    pl.semaphore_wait(barrier, 2 + ntile - 1)
    halos = [halo(step) for step in range(NMOM)]
    for copy in halos[0]:
        copy.start()

    for orbital in range(NORB):
        base = onsite_s if orbital == 0 else onsite_p
        diag[orbital] = (base + diag[orbital]) / energy_scale
    for bond in range(4):
        low[bond] = jnp.bitwise_and(code[bond], LANES - 1)
        code[bond] = lax.shift_right_logical(code[bond], 7) - 1

    def masks():
        return [[jnp.bitwise_and(code[bond], 1 << bit) != 0 for bit in range(3)] for bond in range(4)]

    def gather(ref, *row):
        bits = masks()
        found = [[] for _ in range(4)]
        for group in range(GROUPS):
            source = jnp.broadcast_to(ref[(*row, pl.ds(group, 1), slice(None))], TILE)
            for bond in range(4):
                found[bond].append(lanes_of(source, low[bond]))
        return [pick(bits[bond], found[bond]) for bond in range(4)]

    def gather_ghost(ref, *row):
        below = jnp.broadcast_to(ref[(0, pl.ds(*row, 1), slice(None))], TILE)
        above = jnp.broadcast_to(ref[(1, pl.ds(*row, 1), slice(None))], TILE)
        upper_half = lax.broadcasted_iota(jnp.int32, TILE, 0) >= GROUPS // 2
        return lanes_of(jnp.where(upper_half, above, below), low[0])

    def put_geometry(slot, partner, bonded):
        offset = [partner[axis] - pos[axis] for axis in range(3)]
        distance = jnp.sqrt(offset[0] * offset[0] + offset[1] * offset[1] + offset[2] * offset[2])
        away = distance - bond_length
        radial = jnp.where(bonded, jnp.exp(-0.5 * away * away) / energy_scale, 0.0)
        inverse = 1.0 / jnp.maximum(distance, 1.0)
        geo[slot, 0] = hop_ss * radial
        geo[slot, 1] = hop_sp * radial
        geo[slot, 2] = (hop_pps - hop_ppp) * radial
        geo[slot, 3] = hop_ppp * radial
        for axis in range(3):
            geo[slot, 4 + axis] = offset[axis] * inverse
        geo[slot, 7] = offset[0] * (-1.0 / length_scale)

    def hop(slot, beside):
        along = geo[slot, 4] * beside[1] + geo[slot, 5] * beside[2] + geo[slot, 6] * beside[3]
        mixed = geo[slot, 2] * along - geo[slot, 1] * beside[0]
        result = [geo[slot, 0] * beside[0] + geo[slot, 1] * along]
        for axis in range(3):
            result.append(geo[slot, 4 + axis] * mixed + geo[slot, 3] * beside[1 + axis])
        return result

    partner = [gather(pos, axis) for axis in range(3)]
    for bond in range(4):
        inside = jnp.logical_and(code[bond] >= 0, code[bond] < GROUPS)
        put_geometry(bond, [partner[axis][bond] for axis in range(3)], inside)

    for step in range(NMOM):
        has_b, last = step > 0, step == NMOM - 1

        def inner(vector, carry):
            beside = [gather(a_all, step, orbital * 4 + vector) for orbital in range(NORB)]
            hsum, ksum = [None] * NORB, [None] * NORB
            for bond in range(4):
                term = hop(bond, [beside[orbital][bond] for orbital in range(NORB)])
                drift = geo[bond, 7]
                for orbital in range(NORB):
                    moved = drift * term[orbital]
                    hsum[orbital] = term[orbital] if bond == 0 else hsum[orbital] + term[orbital]
                    ksum[orbital] = moved if bond == 0 else ksum[orbital] + moved
            for orbital in range(NORB):
                if not last:
                    h_a[orbital * 4 + vector] = hsum[orbital]
                k_a[orbital * 4 + vector] = ksum[orbital]
            if has_b:
                beside = [gather(b_all, step - 1, orbital * 4 + vector) for orbital in range(NORB)]
                for bond in range(4):
                    term = hop(bond, [beside[orbital][bond] for orbital in range(NORB)])
                    for orbital in range(NORB):
                        hsum[orbital] = term[orbital] if bond == 0 else hsum[orbital] + term[orbital]
                for orbital in range(NORB):
                    h_b[orbital * 4 + vector] = hsum[orbital]
            return carry

        lax.fori_loop(0, 4, inner, 0)

        for copy in halos[step]:
            copy.wait_recv()
        incoming = ghost0 if step == 0 else ghost.at[step - 1]
        if step == 0:
            outside = jnp.logical_or(code[0] == -1, code[0] == GROUPS)
            put_geometry(4, [gather_ghost(ghost0, 16 + axis) for axis in range(3)], outside)

        def outer(vector, carry):
            rows = [orbital * 4 + vector for orbital in range(NORB)]
            term = hop(4, [gather_ghost(incoming, row) for row in rows])
            drift = geo[4, 7]
            for orbital, row in enumerate(rows):
                moved = k_a[row] + drift * term[orbital]
                if step == 0:
                    b_all[0, row] = moved
                c_all[step, row] = moved
                if not last:
                    value = diag[orbital] * a_all[step, row] + (h_a[row] + term[orbital])
                    if step > 0:
                        value = 2.0 * value - a_all[step - 1, row]
                    a_all[step + 1, row] = value
                    ends = [(value, row)] + ([(moved, 16 + row)] if step == 0 else [])
                    for end, place in ends:
                        send[step, 0, pl.ds(place, 1), :] = end[0:1]
                        send[step, 1, pl.ds(place, 1), :] = end[GROUPS - 1:]
            if has_b:
                term = hop(4, [gather_ghost(incoming, 16 + row) for row in rows])
                for orbital, row in enumerate(rows):
                    value = diag[orbital] * b_all[step - 1, row] + (h_b[row] + term[orbital])
                    if step > 1:
                        value = 2.0 * value - b_all[step - 2, row]
                    b_all[step, row] = value
                    if not last:
                        send[step, 0, pl.ds(16 + row, 1), :] = value[0:1]
                        send[step, 1, pl.ds(16 + row, 1), :] = value[GROUPS - 1:]
            return carry

        lax.fori_loop(0, 4, outer, 0)
        if not last:
            for copy in halos[step + 1]:
                copy.start()

        pairs = [(step, m) for m in range(step + 1)] + [(n, step) for n in range(step)]

        def moments(row, sums):
            b_rows = [b_all[n, row] for n in range(step + 1)]
            c_rows = [c_all[m, row] for m in range(step + 1)]
            return tuple(total + b_rows[n] * c_rows[m] for total, (n, m) in zip(sums, pairs))

        sums = lax.fori_loop(0, 16, moments, tuple(jnp.zeros(TILE, F32) for _ in pairs))
        for (n, m), total in zip(pairs, sums):
            mom[n, m] = total

    copies = []
    for step in range(1, ntile):
        peer = lax.rem(tile + step, ntile)
        copies.append(pltpu.make_async_remote_copy(
            src_ref=mom.at[peer], dst_ref=mom_in.at[step - 1],
            send_sem=mom_send.at[step - 1], recv_sem=mom_recv.at[step - 1],
            device_id={"tile": peer}, device_id_type=MESH,
        ))
    for copy in copies:
        copy.start()
    for copy in copies:
        copy.wait_recv()
    for m in range(NMOM):
        total = mom[tile, m]
        for other in range(ntile - 1):
            total = total + mom_in[other, m]
        out_ref[m] = total * (-1.0 / VECS)
    for group in halos + [copies]:
        for copy in group:
            copy.wait_send()


def body(ndom, ntile, vectors, positions, onsite, neighbors):
    import functools
    rows = NORB * vectors.shape[1]
    hbm = pl.BlockSpec(memory_space=pltpu.HBM)
    tiles = lambda *lead: pltpu.VMEM((*lead, *TILE), F32)
    result = pl.pallas_call(
        functools.partial(kernel, ndom, ntile),
        out_shape=jax.ShapeDtypeStruct((NMOM, *TILE), F32),
        in_specs=[hbm] * 4,
        out_specs=pl.BlockSpec(memory_space=pltpu.VMEM),
        scratch_shapes=[
            pltpu.VMEM(vectors.shape, F32),
            pltpu.VMEM(positions.shape, F32),
            pltpu.VMEM(onsite.shape, F32),
            pltpu.VMEM(neighbors.shape, jnp.int32),
            tiles(3), tiles(4), pltpu.VMEM((4, *TILE), jnp.int32), pltpu.VMEM((4, *TILE), jnp.int32),
            tiles(5, 8), tiles(4, rows), tiles(4, rows), tiles(4, rows),
            tiles(rows), tiles(rows), tiles(rows),
            pltpu.VMEM((2, rows + 3, LANES), F32),
            pltpu.VMEM((3, 2, 2 * rows, LANES), F32),
            pltpu.VMEM((2, rows + 3, LANES), F32),
            pltpu.VMEM((3, 2, 2 * rows, LANES), F32),
            tiles(NMOM, NMOM), tiles(ntile - 1, NMOM),
            pltpu.SemaphoreType.DMA((4,)),
            pltpu.SemaphoreType.DMA((NMOM, 2)),
            pltpu.SemaphoreType.DMA((NMOM, 2)),
            pltpu.SemaphoreType.DMA((ntile - 1,)),
            pltpu.SemaphoreType.DMA((ntile - 1,)),
        ],
        compiler_params=pltpu.CompilerParams(
            collective_id=0, has_side_effects=True, vmem_limit_bytes=16 * 1024 * 1024
        ),
        cost_estimate=pl.CostEstimate(flops=10_000_000, bytes_accessed=150_000, transcendentals=10_000),
    )(vectors, positions, onsite, neighbors)
    return result.reshape(NMOM, GROUPS * LANES)


def solution(mesh):
    import functools
    in_specs = (P(None, "tile", "dom"), P(None, "dom"), P(None, "dom"), P(None, "dom"))
    out_specs = P("tile", "dom")
    local = functools.partial(body, mesh.shape["dom"], mesh.shape["tile"])
    return jax.shard_map(local, mesh=mesh, in_specs=in_specs, out_specs=out_specs, check_vma=False)
```

```python
import jax
import jax.numpy as jnp
from jax import lax
from jax.experimental import pallas as pl
from jax.experimental.pallas import tpu as pltpu
from jax.sharding import PartitionSpec as P

BND = 128
VECS = 16
NMOM = 4
NORB = 4
LANES = 128
GROUPS = 8

onsite_s = -4.2
onsite_p = 1.72
hop_ss = -2.08
hop_sp = 2.48
hop_pps = 2.72
hop_ppp = -0.72
bond_length = 2.35
energy_scale = 16.0
length_scale = 2.0

MESH = pl.DeviceIdType.MESH
F32 = jnp.float32
TILE = (GROUPS, LANES)
POS, DIAG, CODE = 16, 19, 23
UNROLL = True


def lanes_of(source, index):
    return jnp.take_along_axis(source, index, axis=1, mode="promise_in_bounds")


def pick(bits, options):
    for bit in bits:
        options = [jnp.where(bit, options[i + 1], options[i]) for i in range(0, len(options), 2)]
    return options[0]


def kernel(
    ndom, ntile,
    vec_hbm, pos_hbm, ons_hbm, nei_hbm, out_ref,
    vec_in, pos_in, ons_in, nei_in,
    pos, diag, code, low, geo, a_all, b_all, c_all, h_a, h_b, k_a,
    send0, send, ghost0, ghost, local, whole_pos, whole_a, whole_b, strip, mom, mom_in,
    in_sem, halo_send, halo_recv, whole_send, whole_recv, mom_send, mom_recv,
):
    dom, tile = lax.axis_index("dom"), lax.axis_index("tile")
    up, down = lax.rem(dom + 1, ndom), lax.rem(dom + ndom - 1, ndom)

    barrier = pltpu.get_barrier_semaphore()
    for other in (up, down):
        pl.semaphore_signal(barrier, inc=1, device_id={"dom": other}, device_id_type=MESH)
    for step in range(1, ntile):
        peer = lax.rem(tile + step, ntile)
        pl.semaphore_signal(barrier, inc=1, device_id={"tile": peer}, device_id_type=MESH)

    loads = [
        pltpu.make_async_copy(source, target, in_sem.at[i])
        for i, (source, target) in enumerate(
            ((vec_hbm, vec_in), (pos_hbm, pos_in), (nei_hbm, nei_in), (ons_hbm, ons_in))
        )
    ]
    for load in loads:
        load.start()
    for load in loads:
        load.wait()

    for group in range(GROUPS):
        cut = pl.ds(group * LANES, LANES)
        for orbital in range(NORB):
            a_all[0, pl.ds(orbital * 4, 4), group, :] = vec_in[orbital, :, cut]
        pos[:, group, :] = pos_in[:, cut]
        diag[:, group, :] = ons_in[:, cut]
        code[:, group, :] = nei_in[:, cut]
    for orbital in range(NORB):
        base = onsite_s if orbital == 0 else onsite_p
        diag[orbital] = (base + diag[orbital]) / energy_scale
    for side, group in ((0, 0), (1, GROUPS - 1)):
        cut = pl.ds(group * LANES, LANES)
        for orbital in range(NORB):
            send0[side, pl.ds(orbital * 4, 4), :] = vec_in[orbital, :, cut]
        send0[side, pl.ds(POS, 3), :] = pos_in[:, cut]
        send0[side, pl.ds(DIAG, 4), :] = diag[:, group, :]
        send0[side, pl.ds(CODE, 4), :] = nei_in[:, cut].astype(F32)

    def both_ways(sources, target, send_sem, recv_sem):
        return [
            pltpu.make_async_remote_copy(
                src_ref=sources[side], dst_ref=target.at[1 - side],
                send_sem=send_sem.at[side], recv_sem=recv_sem.at[1 - side],
                device_id={"dom": other}, device_id_type=MESH,
            )
            for side, other in ((0, down), (1, up))
        ]

    ends = [
        both_ways((send0.at[0], send0.at[1]), ghost0, halo_send.at[0], halo_recv.at[0]),
        both_ways((send.at[0], send.at[1]), ghost, halo_send.at[1], halo_recv.at[1]),
    ]
    wholes = [
        both_ways((pos, pos), whole_pos, whole_send.at[0], whole_recv.at[0])
        + both_ways((a_all.at[0],) * 2, whole_a.at[0], whole_send.at[1], whole_recv.at[1]),
        both_ways((a_all.at[2],) * 2, whole_a.at[1], whole_send.at[2], whole_recv.at[2])
        + both_ways((b_all.at[1],) * 2, whole_b, whole_send.at[3], whole_recv.at[3]),
    ]

    pl.semaphore_wait(barrier, 2 + ntile - 1)
    for copy in ends[0] + wholes[0]:
        copy.start()

    for bond in range(4):
        low[bond] = jnp.bitwise_and(code[bond], LANES - 1)
        code[bond] = lax.shift_right_logical(code[bond], 7) - 1

    def gather(bond, ref, *row):
        bits = [jnp.bitwise_and(code[bond], 1 << bit) != 0 for bit in range(3)]
        return pick(bits, [
            lanes_of(jnp.broadcast_to(ref[(*row, pl.ds(group, 1), slice(None))], TILE), low[bond])
            for group in range(GROUPS)
        ])

    upper_half = lax.broadcasted_iota(jnp.int32, TILE, 0) >= GROUPS // 2

    def halves(below, above):
        return jnp.where(upper_half, jnp.broadcast_to(above, TILE), jnp.broadcast_to(below, TILE))

    def ends_of(ref, row):
        return halves(ref[0, pl.ds(row, 1), :], ref[1, pl.ds(row, 1), :])

    def gather_ghost(ref, row):
        return lanes_of(ends_of(ref, row), low[0])

    def put_geometry(slot, center, partner, bonded):
        offset = [partner[axis] - center[axis] for axis in range(3)]
        distance = jnp.sqrt(offset[0] * offset[0] + offset[1] * offset[1] + offset[2] * offset[2])
        away = distance - bond_length
        radial = jnp.where(bonded, jnp.exp(-0.5 * away * away) / energy_scale, 0.0)
        inverse = 1.0 / jnp.maximum(distance, 1.0)
        geo[slot, 0] = hop_ss * radial
        geo[slot, 1] = hop_sp * radial
        geo[slot, 2] = (hop_pps - hop_ppp) * radial
        geo[slot, 3] = hop_ppp * radial
        for axis in range(3):
            geo[slot, 4 + axis] = offset[axis] * inverse
        geo[slot, 7] = offset[0] * (-1.0 / length_scale)

    def hop(slot, beside):
        along = geo[slot, 4] * beside[1] + geo[slot, 5] * beside[2] + geo[slot, 6] * beside[3]
        mixed = geo[slot, 2] * along - geo[slot, 1] * beside[0]
        result = [geo[slot, 0] * beside[0] + geo[slot, 1] * along]
        for axis in range(3):
            result.append(geo[slot, 4 + axis] * mixed + geo[slot, 3] * beside[1 + axis])
        return result

    own_pos = [pos[axis] for axis in range(3)]
    for bond in range(4):
        inside = jnp.logical_and(code[bond] >= 0, code[bond] < GROUPS)
        put_geometry(bond, own_pos, [gather(bond, pos, axis) for axis in range(3)], inside)

    def gather_strip(beside, own, row):
        group = strip[1]
        bits = [jnp.bitwise_and(group, 1 << bit) != 0 for bit in range(3)]
        index = strip[0]
        inside = pick(bits, [
            lanes_of(halves(beside[0, row, pl.ds(g, 1), :], beside[1, row, pl.ds(g, 1), :]), index)
            for g in range(GROUPS)
        ])
        mine = lanes_of(halves(own[row, pl.ds(0, 1), :], own[row, pl.ds(GROUPS - 1, 1), :]), index)
        return jnp.where(jnp.logical_or(group == -1, group == GROUPS), mine, inside)

    def bond_sum(value):
        value = value + pltpu.roll(value, 1, 0)
        return value + pltpu.roll(value, 2, 0)

    def put_ends(slot, row, value):
        local[slot, 0, pl.ds(row, 1), :] = value[3:4]
        local[slot, 1, pl.ds(row, 1), :] = value[7:8]

    def strips_first():
        for side in range(2):
            strip[0, pl.ds(side * 4, 4), :] = ghost0[side, pl.ds(CODE, 4), :].astype(jnp.int32)
        number = strip[0]
        group = lax.shift_right_logical(number, 7) - 1
        strip[0] = jnp.bitwise_and(number, LANES - 1)
        strip[1] = group
        center = [ends_of(ghost0, POS + axis) for axis in range(3)]
        put_geometry(5, center, [gather_strip(whole_pos, pos, axis) for axis in range(3)], group < GROUPS + 1)

        def one(vector, carry):
            rows = [orbital * 4 + vector for orbital in range(NORB)]
            term = hop(5, [gather_strip(whole_a.at[0], a_all.at[0], row) for row in rows])
            for orbital, row in enumerate(rows):
                put_ends(0, row, ends_of(ghost0, DIAG + orbital) * ends_of(ghost0, row) + bond_sum(term[orbital]))
                put_ends(0, 16 + row, bond_sum(geo[5, 7] * term[orbital]))
            return carry

        lax.fori_loop(0, 4, one, 0, unroll=UNROLL)

    def strips_second():
        def one(vector, carry):
            rows = [orbital * 4 + vector for orbital in range(NORB)]
            for beside, own, shift in ((whole_a.at[1], a_all.at[2], 0), (whole_b, b_all.at[1], 16)):
                term = hop(5, [gather_strip(beside, own, row) for row in rows])
                for orbital, row in enumerate(rows):
                    value = ends_of(ghost0, DIAG + orbital) * ends_of(ghost, shift + row) + bond_sum(term[orbital])
                    put_ends(1, shift + row, 2.0 * value - ends_of(local.at[0], shift + row))
            return carry

        lax.fori_loop(0, 4, one, 0, unroll=UNROLL)

    for step in range(NMOM):
        has_b, last = step > 0, step == NMOM - 1

        def inner(vector, carry):
            rows = [orbital * 4 + vector for orbital in range(NORB)]
            h_sum, k_sum, hb_sum = [None] * NORB, [None] * NORB, [None] * NORB
            for bond in range(4):
                term = hop(bond, [gather(bond, a_all, step, row) for row in rows])
                drift = geo[bond, 7]
                for orbital in range(NORB):
                    moved = drift * term[orbital]
                    h_sum[orbital] = term[orbital] if bond == 0 else h_sum[orbital] + term[orbital]
                    k_sum[orbital] = moved if bond == 0 else k_sum[orbital] + moved
                if has_b:
                    term = hop(bond, [gather(bond, b_all, step - 1, row) for row in rows])
                    for orbital in range(NORB):
                        hb_sum[orbital] = term[orbital] if bond == 0 else hb_sum[orbital] + term[orbital]
            for orbital, row in enumerate(rows):
                k_a[row] = k_sum[orbital]
                if not last:
                    h_a[row] = h_sum[orbital]
                if has_b:
                    h_b[row] = hb_sum[orbital]
            return carry

        lax.fori_loop(0, 4, inner, 0)

        if step % 2 == 0:
            for copy in ends[step // 2]:
                copy.wait_recv()
            incoming = ghost if step else ghost0
        else:
            for copy in wholes[step // 2]:
                copy.wait_recv()
            (strips_second if step > 1 else strips_first)()
            incoming = local.at[step // 2]
        if step == 0:
            outside = jnp.logical_or(code[0] == -1, code[0] == GROUPS)
            put_geometry(4, own_pos, [gather_ghost(ghost0, POS + axis) for axis in range(3)], outside)

        def outer(vector, carry):
            rows = [orbital * 4 + vector for orbital in range(NORB)]
            term = hop(4, [gather_ghost(incoming, row) for row in rows])
            drift = geo[4, 7]
            for orbital, row in enumerate(rows):
                moved = k_a[row] + drift * term[orbital]
                if step == 0:
                    b_all[0, row] = moved
                c_all[step, row] = moved
                if not last:
                    value = diag[orbital] * a_all[step, row] + (h_a[row] + term[orbital])
                    if step > 0:
                        value = 2.0 * value - a_all[step - 1, row]
                    a_all[step + 1, row] = value
                    if step == 1:
                        send[0, pl.ds(row, 1), :] = value[0:1]
                        send[1, pl.ds(row, 1), :] = value[GROUPS - 1:]
            if has_b:
                term = hop(4, [gather_ghost(incoming, 16 + row) for row in rows])
                for orbital, row in enumerate(rows):
                    value = diag[orbital] * b_all[step - 1, row] + (h_b[row] + term[orbital])
                    if step > 1:
                        value = 2.0 * value - b_all[step - 2, row]
                    b_all[step, row] = value
                    if step == 1:
                        send[0, pl.ds(16 + row, 1), :] = value[0:1]
                        send[1, pl.ds(16 + row, 1), :] = value[GROUPS - 1:]
            return carry

        lax.fori_loop(0, 4, outer, 0, unroll=UNROLL)
        if step == 1:
            for copy in ends[1] + wholes[1]:
                copy.start()

        pairs = [(step, m) for m in range(step + 1)] + [(n, step) for n in range(step)]

        def moments(row, sums):
            b_rows = [b_all[n, row] for n in range(step + 1)]
            c_rows = [c_all[m, row] for m in range(step + 1)]
            return tuple(total + b_rows[n] * c_rows[m] for total, (n, m) in zip(sums, pairs))

        sums = lax.fori_loop(0, 16, moments, tuple(jnp.zeros(TILE, F32) for _ in pairs))
        for (n, m), total in zip(pairs, sums):
            mom[n, m] = total

    copies = []
    for step in range(1, ntile):
        peer = lax.rem(tile + step, ntile)
        copies.append(pltpu.make_async_remote_copy(
            src_ref=mom.at[peer], dst_ref=mom_in.at[step - 1],
            send_sem=mom_send.at[step - 1], recv_sem=mom_recv.at[step - 1],
            device_id={"tile": peer}, device_id_type=MESH,
        ))
    for copy in copies:
        copy.start()
    for copy in copies:
        copy.wait_recv()
    for m in range(NMOM):
        total = mom[tile, m]
        for other in range(ntile - 1):
            total = total + mom_in[other, m]
        out_ref[m] = total * (-1.0 / VECS)
    for group in ends + wholes + [copies]:
        for copy in group:
            copy.wait_send()


def body(ndom, ntile, vectors, positions, onsite, neighbors):
    import functools
    rows = NORB * vectors.shape[1]
    hbm = pl.BlockSpec(memory_space=pltpu.HBM)
    tiles = lambda *lead: pltpu.VMEM((*lead, *TILE), F32)
    result = pl.pallas_call(
        functools.partial(kernel, ndom, ntile),
        out_shape=jax.ShapeDtypeStruct((NMOM, *TILE), F32),
        in_specs=[hbm] * 4,
        out_specs=pl.BlockSpec(memory_space=pltpu.VMEM),
        scratch_shapes=[
            pltpu.VMEM(vectors.shape, F32),
            pltpu.VMEM(positions.shape, F32),
            pltpu.VMEM(onsite.shape, F32),
            pltpu.VMEM(neighbors.shape, jnp.int32),
            tiles(3), tiles(4), pltpu.VMEM((4, *TILE), jnp.int32), pltpu.VMEM((4, *TILE), jnp.int32),
            tiles(6, 8), tiles(4, rows), tiles(4, rows), tiles(4, rows),
            tiles(rows), tiles(rows), tiles(rows),
            pltpu.VMEM((2, CODE + 4, LANES), F32),
            pltpu.VMEM((2, 2 * rows, LANES), F32),
            pltpu.VMEM((2, CODE + 4, LANES), F32),
            pltpu.VMEM((2, 2 * rows, LANES), F32),
            pltpu.VMEM((2, 2, 2 * rows, LANES), F32),
            tiles(2, 3), tiles(2, 2, rows), tiles(2, rows),
            pltpu.VMEM((2, *TILE), jnp.int32),
            tiles(NMOM, NMOM), tiles(ntile - 1, NMOM),
            pltpu.SemaphoreType.DMA((4,)),
            pltpu.SemaphoreType.DMA((2, 2)),
            pltpu.SemaphoreType.DMA((2, 2)),
            pltpu.SemaphoreType.DMA((4, 2)),
            pltpu.SemaphoreType.DMA((4, 2)),
            pltpu.SemaphoreType.DMA((ntile - 1,)),
            pltpu.SemaphoreType.DMA((ntile - 1,)),
        ],
        compiler_params=pltpu.CompilerParams(
            collective_id=0, has_side_effects=True, vmem_limit_bytes=60 * 1024 * 1024
        ),
        cost_estimate=pl.CostEstimate(flops=10_000_000, bytes_accessed=150_000, transcendentals=10_000),
    )(vectors, positions, onsite, neighbors)
    return result.reshape(NMOM, GROUPS * LANES)


def solution(mesh):
    import functools
    in_specs = (P(None, "tile", "dom"), P(None, "dom"), P(None, "dom"), P(None, "dom"))
    out_specs = P("tile", "dom")
    local = functools.partial(body, mesh.shape["dom"], mesh.shape["tile"])
    return jax.shard_map(local, mesh=mesh, in_specs=in_specs, out_specs=out_specs, check_vma=False)
```

```python
import jax
import jax.numpy as jnp
from jax import lax
from jax.experimental import pallas as pl
from jax.experimental.pallas import tpu as pltpu
from jax.sharding import PartitionSpec as P

BND = 128
VECS = 16
NMOM = 4
NORB = 4
LANES = 128
GROUPS = 8

onsite_s = -4.2
onsite_p = 1.72
hop_ss = -2.08
hop_sp = 2.48
hop_pps = 2.72
hop_ppp = -0.72
bond_length = 2.35
energy_scale = 16.0
length_scale = 2.0

MESH = pl.DeviceIdType.MESH
F32 = jnp.float32
TILE = (GROUPS, LANES)
POS, CODE = 16, 19


def lanes_of(source, index):
    return jnp.take_along_axis(source, index, axis=1, mode="promise_in_bounds")


def pick(bits, options):
    for bit in bits:
        options = [jnp.where(bit, options[i + 1], options[i]) for i in range(0, len(options), 2)]
    return options[0]


def kernel(
    ndom, ntile,
    vec_hbm, pos_hbm, ons_hbm, nei_hbm, out_ref,
    vec_in, pos_in, ons_in, nei_in,
    pos, diag, code, low, geo, a_all, b_all, c_all, h_a, h_b, k_a, change, tip,
    send0, send, ghost0, ghost, mom, mom_in,
    in_sem, halo_send, halo_recv, mom_send, mom_recv,
):
    dom, tile = lax.axis_index("dom"), lax.axis_index("tile")
    up, down = lax.rem(dom + 1, ndom), lax.rem(dom + ndom - 1, ndom)

    barrier = pltpu.get_barrier_semaphore()
    for other in (up, down):
        pl.semaphore_signal(barrier, inc=1, device_id={"dom": other}, device_id_type=MESH)
    for step in range(1, ntile):
        peer = lax.rem(tile + step, ntile)
        pl.semaphore_signal(barrier, inc=1, device_id={"tile": peer}, device_id_type=MESH)

    loads = [
        pltpu.make_async_copy(source, target, in_sem.at[i])
        for i, (source, target) in enumerate(
            ((vec_hbm, vec_in), (pos_hbm, pos_in), (nei_hbm, nei_in), (ons_hbm, ons_in))
        )
    ]
    for load in loads:
        load.start()
    for load in loads:
        load.wait()

    for group in range(GROUPS):
        cut = pl.ds(group * LANES, LANES)
        for orbital in range(NORB):
            a_all[0, pl.ds(orbital * 4, 4), group, :] = vec_in[orbital, :, cut]
        pos[:, group, :] = pos_in[:, cut]
        diag[:, group, :] = ons_in[:, cut]
        code[:, group, :] = nei_in[:, cut]
    for orbital in range(NORB):
        base = onsite_s if orbital == 0 else onsite_p
        diag[orbital] = (base + diag[orbital]) / energy_scale
    for side, group in ((0, 0), (1, GROUPS - 1)):
        cut = pl.ds(group * LANES, LANES)
        for orbital in range(NORB):
            send0[side, pl.ds(orbital * 4, 4), :] = vec_in[orbital, :, cut]
        send0[side, pl.ds(POS, 3), :] = pos_in[:, cut]
        send0[side, pl.ds(CODE, 1), :] = nei_in[0:1, cut].astype(F32)

    def both_ways(sources, target, send_sem, recv_sem):
        return [
            pltpu.make_async_remote_copy(
                src_ref=sources[side], dst_ref=target.at[1 - side],
                send_sem=send_sem.at[side], recv_sem=recv_sem.at[1 - side],
                device_id={"dom": other}, device_id_type=MESH,
            )
            for side, other in ((0, down), (1, up))
        ]

    halos = [both_ways((send0.at[0], send0.at[1]), ghost0, halo_send.at[0], halo_recv.at[0])] + [
        both_ways((send.at[i, 0], send.at[i, 1]), ghost.at[i], halo_send.at[i + 1], halo_recv.at[i + 1])
        for i in range(3)
    ]

    pl.semaphore_wait(barrier, 2 + ntile - 1)
    for copy in halos[0]:
        copy.start()

    for bond in range(4):
        low[bond] = jnp.bitwise_and(code[bond], LANES - 1)
        code[bond] = lax.shift_right_logical(code[bond], 7) - 1

    def gather(bond, ref, *row):
        bits = [jnp.bitwise_and(code[bond], 1 << bit) != 0 for bit in range(3)]
        return pick(bits, [
            lanes_of(jnp.broadcast_to(ref[(*row, pl.ds(group, 1), slice(None))], TILE), low[bond])
            for group in range(GROUPS)
        ])

    upper_half = lax.broadcasted_iota(jnp.int32, TILE, 0) >= GROUPS // 2

    def halves(below, above):
        return jnp.where(upper_half, jnp.broadcast_to(above, TILE), jnp.broadcast_to(below, TILE))

    def ends_of(ref, row):
        return halves(ref[0, pl.ds(row, 1), :], ref[1, pl.ds(row, 1), :])

    def gather_ghost(ref, row):
        return lanes_of(ends_of(ref, row), low[0])

    def put_geometry(slot, center, partner, bonded):
        offset = [partner[axis] - center[axis] for axis in range(3)]
        distance = jnp.sqrt(offset[0] * offset[0] + offset[1] * offset[1] + offset[2] * offset[2])
        away = distance - bond_length
        radial = jnp.where(bonded, jnp.exp(-0.5 * away * away) / energy_scale, 0.0)
        inverse = 1.0 / jnp.maximum(distance, 1.0)
        geo[slot, 0] = hop_ss * radial
        geo[slot, 1] = hop_sp * radial
        geo[slot, 2] = (hop_pps - hop_ppp) * radial
        geo[slot, 3] = hop_ppp * radial
        for axis in range(3):
            geo[slot, 4 + axis] = offset[axis] * inverse
        geo[slot, 7] = offset[0] * (-1.0 / length_scale)

    def hop(slot, beside):
        along = geo[slot, 4] * beside[1] + geo[slot, 5] * beside[2] + geo[slot, 6] * beside[3]
        mixed = geo[slot, 2] * along - geo[slot, 1] * beside[0]
        result = [geo[slot, 0] * beside[0] + geo[slot, 1] * along]
        for axis in range(3):
            result.append(geo[slot, 4 + axis] * mixed + geo[slot, 3] * beside[1 + axis])
        return result

    own_pos = [pos[axis] for axis in range(3)]
    for bond in range(4):
        inside = jnp.logical_and(code[bond] >= 0, code[bond] < GROUPS)
        put_geometry(bond, own_pos, [gather(bond, pos, axis) for axis in range(3)], inside)

    def rows_of(vector):
        return [orbital * 4 + vector for orbital in range(NORB)]

    def add(total, term):
        return term if total is None else [x + y for x, y in zip(total, term)]

    def put_ends(slot, row, value):
        send[slot, 0, pl.ds(row, 1), :] = value[0:1]
        send[slot, 1, pl.ds(row, 1), :] = value[GROUPS - 1:]

    def interior(found, want_h, want_k):
        h_sum = k_sum = None
        for bond in range(4):
            term = hop(bond, found(bond))
            if want_h:
                h_sum = add(h_sum, term)
            if want_k:
                drift = geo[bond, 7]
                k_sum = add(k_sum, [drift * x for x in term])
        return h_sum, k_sum

    def gather_ends(bond, row):
        group, index = code[bond], low[bond]
        first = lanes_of(jnp.broadcast_to(change[row, pl.ds(0, 1), :], TILE), index)
        last = lanes_of(jnp.broadcast_to(change[row, pl.ds(GROUPS - 1, 1), :], TILE), index)
        return jnp.where(group == 0, first, jnp.where(group == GROUPS - 1, last, 0.0))

    def gather_mine(ref, row):
        return lanes_of(halves(ref[row, pl.ds(0, 1), :], ref[row, pl.ds(GROUPS - 1, 1), :]), low[4])

    def loop(function):
        lax.fori_loop(0, 4, lambda vector, carry: function(vector) or carry, 0)

    def loop_flat(function):
        for vector in range(4):
            function(vector)

    def moments_of(step):
        pairs = [(step, m) for m in range(step + 1)] + [(n, step) for n in range(step)]

        def moments(row, sums):
            b_rows = [b_all[n, row] for n in range(step + 1)]
            c_rows = [c_all[m, row] if m else b_rows[0] for m in range(step + 1)]
            return tuple(total + b_rows[n] * c_rows[m] for total, (n, m) in zip(sums, pairs))

        sums = lax.fori_loop(0, 16, moments, tuple(jnp.zeros(TILE, F32) for _ in pairs), unroll=4)
        for (n, m), total in zip(pairs, sums):
            mom[n, m] = total

    def first(vector):
        rows = rows_of(vector)
        h_sum, k_sum = interior(lambda bond: [gather(bond, a_all, 0, row) for row in rows], True, True)
        for orbital, row in enumerate(rows):
            value = diag[orbital] * a_all[0, row] + h_sum[orbital]
            a_all[1, row] = value
            b_all[0, row] = k_sum[orbital]
            put_ends(0, row, value)
            put_ends(0, 16 + row, k_sum[orbital])

    def second(vector):
        rows = rows_of(vector)
        h_sum, k_sum = interior(lambda bond: [gather(bond, a_all, 1, row) for row in rows], True, True)
        hb_sum, _ = interior(lambda bond: [gather(bond, b_all, 0, row) for row in rows], True, False)
        for orbital, row in enumerate(rows):
            h_a[row], k_a[row], h_b[row] = h_sum[orbital], k_sum[orbital], hb_sum[orbital]

    loop(first)
    for copy in halos[1]:
        copy.start()
    loop(second)

    for copy in halos[0]:
        copy.wait_recv()
    outside = jnp.logical_or(code[0] == -1, code[0] == GROUPS)
    put_geometry(4, own_pos, [gather_ghost(ghost0, POS + axis) for axis in range(3)], outside)
    number = ends_of(ghost0, CODE).astype(jnp.int32)
    group = lax.shift_right_logical(number, 7) - 1
    low[4] = jnp.bitwise_and(number, LANES - 1)
    put_geometry(
        5, [ends_of(ghost0, POS + axis) for axis in range(3)], [gather_mine(pos, axis) for axis in range(3)],
        jnp.logical_or(group == -1, group == GROUPS),
    )

    def third(vector):
        rows = rows_of(vector)
        term = hop(4, [gather_ghost(ghost0, row) for row in rows])
        mine = hop(5, [gather_mine(a_all.at[0], row) for row in rows])
        for orbital, row in enumerate(rows):
            moved = geo[4, 7] * term[orbital]
            change[row], change[16 + row] = term[orbital], moved
            a_all[1, row] = a_all[1, row] + term[orbital]
            b_all[0, row] = b_all[0, row] + moved
            tip[row], tip[16 + row] = mine[orbital], geo[5, 7] * mine[orbital]

    def fourth(vector):
        rows = rows_of(vector)
        h_sum, k_sum = interior(lambda bond: [gather_ends(bond, row) for row in rows], True, True)
        hb_sum, _ = interior(lambda bond: [gather_ends(bond, 16 + row) for row in rows], True, False)
        for orbital, row in enumerate(rows):
            h_a[row], k_a[row] = h_a[row] + h_sum[orbital], k_a[row] + k_sum[orbital]
            h_b[row] = h_b[row] + hb_sum[orbital]

    def ghost_terms(vector, slot):
        rows = rows_of(vector)
        return [
            hop(4, [lanes_of(tip[shift + row] + ends_of(ghost.at[slot], shift + row), low[0]) for row in rows])
            for shift in (0, 16)
        ]

    def fifth(vector):
        term, term_b = ghost_terms(vector, 0)
        for orbital, row in enumerate(rows_of(vector)):
            c_all[1, row] = k_a[row] + geo[4, 7] * term[orbital]
            value = 2.0 * (diag[orbital] * a_all[1, row] + (h_a[row] + term[orbital])) - a_all[0, row]
            value_b = diag[orbital] * b_all[0, row] + (h_b[row] + term_b[orbital])
            a_all[2, row], b_all[1, row] = value, value_b
            put_ends(1, row, value)
            put_ends(1, 16 + row, value_b)

    loop_flat(third)
    loop_flat(fourth)
    for copy in halos[1]:
        copy.wait_recv()
    loop_flat(fifth)
    for copy in halos[2]:
        copy.start()

    def sixth(vector):
        rows = rows_of(vector)
        h_sum, k_sum = interior(lambda bond: [gather(bond, a_all, 2, row) for row in rows], True, True)
        hb_sum, _ = interior(lambda bond: [gather(bond, b_all, 1, row) for row in rows], True, False)
        for orbital, row in enumerate(rows):
            value = 2.0 * (diag[orbital] * a_all[2, row] + h_sum[orbital]) - a_all[1, row]
            value_b = 2.0 * (diag[orbital] * b_all[1, row] + hb_sum[orbital]) - b_all[0, row]
            a_all[3, row], b_all[2, row], c_all[2, row] = value, value_b, k_sum[orbital]
            put_ends(2, row, value)
            put_ends(2, 16 + row, value_b)

    def seventh(vector):
        rows = rows_of(vector)
        _, k_sum = interior(lambda bond: [gather(bond, a_all, 3, row) for row in rows], False, True)
        hb_sum, _ = interior(lambda bond: [gather(bond, b_all, 2, row) for row in rows], True, False)
        mine = hop(5, [gather_mine(a_all.at[2], row) for row in rows])
        mine_b = hop(5, [gather_mine(b_all.at[1], row) for row in rows])
        for orbital, row in enumerate(rows):
            k_a[row], h_b[row] = k_sum[orbital], hb_sum[orbital]
            tip[row], tip[16 + row] = 2.0 * mine[orbital], 2.0 * mine_b[orbital]

    loop(sixth)
    for copy in halos[3]:
        copy.start()
    loop(seventh)
    moments_of(0)
    moments_of(1)

    for copy in halos[2]:
        copy.wait_recv()

    def eighth(vector):
        rows = rows_of(vector)
        term = hop(4, [gather_ghost(ghost.at[1], row) for row in rows])
        term_b = hop(4, [gather_ghost(ghost.at[1], 16 + row) for row in rows])
        for orbital, row in enumerate(rows):
            change[row], change[16 + row] = 2.0 * term[orbital], 2.0 * term_b[orbital]
            c_all[2, row] = c_all[2, row] + geo[4, 7] * term[orbital]
            b_all[2, row] = b_all[2, row] + 2.0 * term_b[orbital]

    def ninth(vector):
        rows = rows_of(vector)
        _, k_sum = interior(lambda bond: [gather_ends(bond, row) for row in rows], False, True)
        hb_sum, _ = interior(lambda bond: [gather_ends(bond, 16 + row) for row in rows], True, False)
        for orbital, row in enumerate(rows):
            k_a[row], h_b[row] = k_a[row] + k_sum[orbital], h_b[row] + hb_sum[orbital]

    def tenth(vector):
        term, term_b = ghost_terms(vector, 2)
        for orbital, row in enumerate(rows_of(vector)):
            c_all[3, row] = k_a[row] + geo[4, 7] * term[orbital]
            b_all[3, row] = 2.0 * (diag[orbital] * b_all[2, row] + (h_b[row] + term_b[orbital])) - b_all[1, row]

    loop_flat(eighth)
    loop_flat(ninth)
    moments_of(2)
    for copy in halos[3]:
        copy.wait_recv()
    loop_flat(tenth)
    moments_of(3)

    copies = []
    for step in range(1, ntile):
        peer = lax.rem(tile + step, ntile)
        copies.append(pltpu.make_async_remote_copy(
            src_ref=mom.at[peer], dst_ref=mom_in.at[step - 1],
            send_sem=mom_send.at[step - 1], recv_sem=mom_recv.at[step - 1],
            device_id={"tile": peer}, device_id_type=MESH,
        ))
    for copy in copies:
        copy.start()
    for copy in copies:
        copy.wait_recv()
    for m in range(NMOM):
        total = mom[tile, m]
        for other in range(ntile - 1):
            total = total + mom_in[other, m]
        out_ref[m] = total * (-1.0 / VECS)
    for group in halos + [copies]:
        for copy in group:
            copy.wait_send()


def body(ndom, ntile, vectors, positions, onsite, neighbors):
    import functools
    rows = NORB * vectors.shape[1]
    hbm = pl.BlockSpec(memory_space=pltpu.HBM)
    tiles = lambda *lead: pltpu.VMEM((*lead, *TILE), F32)
    result = pl.pallas_call(
        functools.partial(kernel, ndom, ntile),
        out_shape=jax.ShapeDtypeStruct((NMOM, *TILE), F32),
        in_specs=[hbm] * 4,
        out_specs=pl.BlockSpec(memory_space=pltpu.VMEM),
        scratch_shapes=[
            pltpu.VMEM(vectors.shape, F32),
            pltpu.VMEM(positions.shape, F32),
            pltpu.VMEM(onsite.shape, F32),
            pltpu.VMEM(neighbors.shape, jnp.int32),
            tiles(3), tiles(4), pltpu.VMEM((4, *TILE), jnp.int32), pltpu.VMEM((5, *TILE), jnp.int32),
            tiles(6, 8), tiles(4, rows), tiles(4, rows), tiles(4, rows),
            tiles(rows), tiles(rows), tiles(rows), tiles(2 * rows), tiles(2 * rows),
            pltpu.VMEM((2, CODE + 1, LANES), F32),
            pltpu.VMEM((3, 2, 2 * rows, LANES), F32),
            pltpu.VMEM((2, CODE + 1, LANES), F32),
            pltpu.VMEM((3, 2, 2 * rows, LANES), F32),
            tiles(NMOM, NMOM), tiles(ntile - 1, NMOM),
            pltpu.SemaphoreType.DMA((4,)),
            pltpu.SemaphoreType.DMA((4, 2)),
            pltpu.SemaphoreType.DMA((4, 2)),
            pltpu.SemaphoreType.DMA((ntile - 1,)),
            pltpu.SemaphoreType.DMA((ntile - 1,)),
        ],
        compiler_params=pltpu.CompilerParams(
            collective_id=0, has_side_effects=True, vmem_limit_bytes=60 * 1024 * 1024
        ),
        cost_estimate=pl.CostEstimate(flops=10_000_000, bytes_accessed=150_000, transcendentals=10_000),
    )(vectors, positions, onsite, neighbors)
    return result.reshape(NMOM, GROUPS * LANES)


def solution(mesh):
    import functools
    in_specs = (P(None, "tile", "dom"), P(None, "dom"), P(None, "dom"), P(None, "dom"))
    out_specs = P("tile", "dom")
    local = functools.partial(body, mesh.shape["dom"], mesh.shape["tile"])
    return jax.shard_map(local, mesh=mesh, in_specs=in_specs, out_specs=out_specs, check_vma=False)
```

```python
import jax
import jax.numpy as jnp
from jax import lax
from jax.experimental import pallas as pl
from jax.experimental.pallas import tpu as pltpu
from jax.sharding import PartitionSpec as P

BND = 128
VECS = 16
NMOM = 4
NORB = 4
LANES = 128
GROUPS = 8

onsite_s = -4.2
onsite_p = 1.72
hop_ss = -2.08
hop_sp = 2.48
hop_pps = 2.72
hop_ppp = -0.72
bond_length = 2.35
energy_scale = 16.0
length_scale = 2.0

MESH = pl.DeviceIdType.MESH
F32 = jnp.float32
TILE = (GROUPS, LANES)
POS, CODE = 16, 19


def lanes_of(source, index):
    return jnp.take_along_axis(source, index, axis=1, mode="promise_in_bounds")


def pick(bits, options):
    for bit in bits:
        options = [jnp.where(bit, options[i + 1], options[i]) for i in range(0, len(options), 2)]
    return options[0]


def kernel(
    ndom, ntile,
    vec_hbm, pos_hbm, ons_hbm, nei_hbm, out_ref,
    vec_in, pos_in, ons_in, nei_in,
    pos, diag, code, low, geo, a_all, b_all, c_all, h_a, h_b, k_a, change, tip,
    send0, send, ghost0, ghost, mom, mom_in,
    in_sem, halo_send, halo_recv, mom_send, mom_recv,
):
    dom, tile = lax.axis_index("dom"), lax.axis_index("tile")
    up, down = lax.rem(dom + 1, ndom), lax.rem(dom + ndom - 1, ndom)

    barrier = pltpu.get_barrier_semaphore()
    for other in (up, down):
        pl.semaphore_signal(barrier, inc=1, device_id={"dom": other}, device_id_type=MESH)
    for step in range(1, ntile):
        peer = lax.rem(tile + step, ntile)
        pl.semaphore_signal(barrier, inc=1, device_id={"tile": peer}, device_id_type=MESH)

    loads = [
        pltpu.make_async_copy(source, target, in_sem.at[i])
        for i, (source, target) in enumerate(
            ((vec_hbm, vec_in), (pos_hbm, pos_in), (nei_hbm, nei_in), (ons_hbm, ons_in))
        )
    ]
    for load in loads:
        load.start()
    for load in loads:
        load.wait()

    for group in range(GROUPS):
        cut = pl.ds(group * LANES, LANES)
        for orbital in range(NORB):
            a_all[0, pl.ds(orbital * 4, 4), group, :] = vec_in[orbital, :, cut]
        pos[:, group, :] = pos_in[:, cut]
        diag[pl.ds(0, 4), group, :] = ons_in[:, cut]
        code[pl.ds(0, 4), group, :] = nei_in[:, cut]
    for orbital in range(NORB):
        base = onsite_s if orbital == 0 else onsite_p
        diag[orbital] = (base + diag[orbital]) / energy_scale
    for side, group in ((0, 0), (1, GROUPS - 1)):
        cut = pl.ds(group * LANES, LANES)
        for orbital in range(NORB):
            send0[side, pl.ds(orbital * 4, 4), :] = vec_in[orbital, :, cut]
        send0[side, pl.ds(POS, 3), :] = pos_in[:, cut]
        send0[side, pl.ds(CODE, 1), :] = nei_in[0:1, cut].astype(F32)

    def both_ways(sources, target, send_sem, recv_sem):
        return [
            pltpu.make_async_remote_copy(
                src_ref=sources[side], dst_ref=target.at[1 - side],
                send_sem=send_sem.at[side], recv_sem=recv_sem.at[1 - side],
                device_id={"dom": other}, device_id_type=MESH,
            )
            for side, other in ((0, down), (1, up))
        ]

    halos = [both_ways((send0.at[0], send0.at[1]), ghost0, halo_send.at[0], halo_recv.at[0])] + [
        both_ways((send.at[i, 0], send.at[i, 1]), ghost.at[i], halo_send.at[i + 1], halo_recv.at[i + 1])
        for i in range(3)
    ]

    for bond in range(4):
        low[bond] = jnp.bitwise_and(code[bond], LANES - 1)
        code[bond] = lax.shift_right_logical(code[bond], 7) - 1

    def gather(bond, ref, *row):
        bits = [jnp.bitwise_and(code[bond], 1 << bit) != 0 for bit in range(3)]
        return pick(bits, [
            lanes_of(jnp.broadcast_to(ref[(*row, pl.ds(group, 1), slice(None))], TILE), low[bond])
            for group in range(GROUPS)
        ])

    upper_half = lax.broadcasted_iota(jnp.int32, TILE, 0) >= GROUPS // 2

    def halves(below, above):
        return jnp.where(upper_half, jnp.broadcast_to(above, TILE), jnp.broadcast_to(below, TILE))

    def ends_of(ref, row):
        return halves(ref[0, pl.ds(row, 1), :], ref[1, pl.ds(row, 1), :])

    def gather_ghost(ref, row):
        return lanes_of(ends_of(ref, row), low[0])

    def put_geometry(slot, center, partner, bonded):
        offset = [partner[axis] - center[axis] for axis in range(3)]
        distance = jnp.sqrt(offset[0] * offset[0] + offset[1] * offset[1] + offset[2] * offset[2])
        away = distance - bond_length
        radial = jnp.where(bonded, jnp.exp(-0.5 * away * away) / energy_scale, 0.0)
        inverse = 1.0 / jnp.maximum(distance, 1.0)
        geo[slot, 0] = hop_ss * radial
        geo[slot, 1] = hop_sp * radial
        geo[slot, 2] = (hop_pps - hop_ppp) * radial
        geo[slot, 3] = hop_ppp * radial
        for axis in range(3):
            geo[slot, 4 + axis] = offset[axis] * inverse
        geo[slot, 7] = offset[0] * (-1.0 / length_scale)

    def hop(slot, beside):
        along = geo[slot, 4] * beside[1] + geo[slot, 5] * beside[2] + geo[slot, 6] * beside[3]
        mixed = geo[slot, 2] * along - geo[slot, 1] * beside[0]
        result = [geo[slot, 0] * beside[0] + geo[slot, 1] * along]
        for axis in range(3):
            result.append(geo[slot, 4 + axis] * mixed + geo[slot, 3] * beside[1 + axis])
        return result

    own_pos = [pos[axis] for axis in range(3)]
    for bond in range(4):
        inside = jnp.logical_and(code[bond] >= 0, code[bond] < GROUPS)
        put_geometry(bond, own_pos, [gather(bond, pos, axis) for axis in range(3)], inside)

    def put_own_ends():
        for side, group in ((0, 0), (1, GROUPS - 1)):
            for bond in range(4):
                place = pl.ds(side * 4 + bond, 1)
                low[5, place, :] = low[bond, pl.ds(group, 1), :]
                code[4, place, :] = code[bond, pl.ds(group, 1), :]
                for entry in range(7):
                    geo[6, entry, place, :] = geo[bond, entry, pl.ds(group, 1), :]
        for orbital in range(NORB):
            diag[4 + orbital] = halves(diag[orbital, pl.ds(0, 1), :], diag[orbital, pl.ds(GROUPS - 1, 1), :])

    def bond_sum(value):
        value = value + pltpu.roll(value, 1, 0)
        return value + pltpu.roll(value, 2, 0)

    def own_ends(ref, row):
        return halves(ref[row, pl.ds(0, 1), :], ref[row, pl.ds(GROUPS - 1, 1), :])

    def next_ends(current, past, row_shift):
        bits = [jnp.bitwise_and(code[4], 1 << bit) != 0 for bit in range(3)]
        for vector in range(4):
            rows = rows_of(vector)
            term = hop(6, [
                pick(bits, [
                    lanes_of(jnp.broadcast_to(current[row, pl.ds(group, 1), :], TILE), low[5])
                    for group in range(GROUPS)
                ])
                for row in rows
            ])
            for orbital, row in enumerate(rows):
                value = diag[4 + orbital] * own_ends(current, row) + bond_sum(term[orbital])
                value = 2.0 * value - own_ends(past, row)
                send[2, 0, pl.ds(row_shift + row, 1), :] = value[3:4]
                send[2, 1, pl.ds(row_shift + row, 1), :] = value[7:8]

    def rows_of(vector):
        return [orbital * 4 + vector for orbital in range(NORB)]

    def add(total, term):
        return term if total is None else [x + y for x, y in zip(total, term)]

    def put_ends(slot, row, value):
        send[slot, 0, pl.ds(row, 1), :] = value[0:1]
        send[slot, 1, pl.ds(row, 1), :] = value[GROUPS - 1:]

    def interior(found, want_h, want_k):
        h_sum = k_sum = None
        for bond in range(4):
            term = hop(bond, found(bond))
            if want_h:
                h_sum = add(h_sum, term)
            if want_k:
                drift = geo[bond, 7]
                k_sum = add(k_sum, [drift * x for x in term])
        return h_sum, k_sum

    def gather_ends(bond, row):
        group, index = code[bond], low[bond]
        first = lanes_of(jnp.broadcast_to(change[row, pl.ds(0, 1), :], TILE), index)
        last = lanes_of(jnp.broadcast_to(change[row, pl.ds(GROUPS - 1, 1), :], TILE), index)
        return jnp.where(group == 0, first, jnp.where(group == GROUPS - 1, last, 0.0))

    def gather_mine(ref, row):
        return lanes_of(halves(ref[row, pl.ds(0, 1), :], ref[row, pl.ds(GROUPS - 1, 1), :]), low[4])

    def loop(function):
        lax.fori_loop(0, 4, lambda vector, carry: function(vector) or carry, 0)

    def loop_flat(function):
        for vector in range(4):
            function(vector)

    def moments_of(step):
        pairs = [(step, m) for m in range(step + 1)] + [(n, step) for n in range(step)]

        def moments(row, sums):
            b_rows = [b_all[n, row] for n in range(step + 1)]
            c_rows = [c_all[m, row] if m else b_rows[0] for m in range(step + 1)]
            return tuple(total + b_rows[n] * c_rows[m] for total, (n, m) in zip(sums, pairs))

        sums = lax.fori_loop(0, 16, moments, tuple(jnp.zeros(TILE, F32) for _ in pairs), unroll=4)
        for (n, m), total in zip(pairs, sums):
            mom[n, m] = total

    def to_peer(step, part, rows):
        peer = lax.rem(tile + step, ntile)
        return pltpu.make_async_remote_copy(
            src_ref=mom.at[peer, rows], dst_ref=mom_in.at[step - 1, rows],
            send_sem=mom_send.at[part, step - 1], recv_sem=mom_recv.at[part, step - 1],
            device_id={"tile": peer}, device_id_type=MESH,
        )

    others = range(1, ntile)
    owns_last = [lax.rem(tile + step, ntile) == NMOM - 1 for step in others]
    early = [to_peer(step, 0, pl.ds(0, NMOM - 1)) for step in others]
    late_one = [to_peer(step, 1, pl.ds(NMOM - 1, 1)) for step in others]
    late_all = [to_peer(step, 2, pl.ds(0, NMOM)) for step in others]

    def first(vector):
        rows = rows_of(vector)
        h_sum, k_sum = interior(lambda bond: [gather(bond, a_all, 0, row) for row in rows], True, True)
        for orbital, row in enumerate(rows):
            value = diag[orbital] * a_all[0, row] + h_sum[orbital]
            a_all[1, row] = value
            b_all[0, row] = k_sum[orbital]
            put_ends(0, row, value)
            put_ends(0, 16 + row, k_sum[orbital])

    def second(vector):
        rows = rows_of(vector)
        h_sum, k_sum = interior(lambda bond: [gather(bond, a_all, 1, row) for row in rows], True, True)
        hb_sum, _ = interior(lambda bond: [gather(bond, b_all, 0, row) for row in rows], True, False)
        for orbital, row in enumerate(rows):
            h_a[row], k_a[row], h_b[row] = h_sum[orbital], k_sum[orbital], hb_sum[orbital]

    loop(first)
    pl.semaphore_wait(barrier, 2 + ntile - 1)
    for copy in halos[0] + halos[1]:
        copy.start()
    loop(second)
    put_own_ends()

    for copy in halos[0]:
        copy.wait_recv()
    outside = jnp.logical_or(code[0] == -1, code[0] == GROUPS)
    put_geometry(4, own_pos, [gather_ghost(ghost0, POS + axis) for axis in range(3)], outside)
    number = ends_of(ghost0, CODE).astype(jnp.int32)
    group = lax.shift_right_logical(number, 7) - 1
    low[4] = jnp.bitwise_and(number, LANES - 1)
    put_geometry(
        5, [ends_of(ghost0, POS + axis) for axis in range(3)], [gather_mine(pos, axis) for axis in range(3)],
        jnp.logical_or(group == -1, group == GROUPS),
    )

    def third(vector):
        rows = rows_of(vector)
        term = hop(4, [gather_ghost(ghost0, row) for row in rows])
        mine = hop(5, [gather_mine(a_all.at[0], row) for row in rows])
        for orbital, row in enumerate(rows):
            moved = geo[4, 7] * term[orbital]
            change[row], change[16 + row] = term[orbital], moved
            a_all[1, row] = a_all[1, row] + term[orbital]
            b_all[0, row] = b_all[0, row] + moved
            tip[row], tip[16 + row] = mine[orbital], geo[5, 7] * mine[orbital]

    def fourth(vector):
        rows = rows_of(vector)
        h_sum, k_sum = interior(lambda bond: [gather_ends(bond, row) for row in rows], True, True)
        hb_sum, _ = interior(lambda bond: [gather_ends(bond, 16 + row) for row in rows], True, False)
        for orbital, row in enumerate(rows):
            h_a[row], k_a[row] = h_a[row] + h_sum[orbital], k_a[row] + k_sum[orbital]
            h_b[row] = h_b[row] + hb_sum[orbital]

    def ghost_terms(vector, slot):
        rows = rows_of(vector)
        return [
            hop(4, [lanes_of(tip[shift + row] + ends_of(ghost.at[slot], shift + row), low[0]) for row in rows])
            for shift in (0, 16)
        ]

    def fifth(vector):
        term, term_b = ghost_terms(vector, 0)
        for orbital, row in enumerate(rows_of(vector)):
            c_all[1, row] = k_a[row] + geo[4, 7] * term[orbital]
            value = 2.0 * (diag[orbital] * a_all[1, row] + (h_a[row] + term[orbital])) - a_all[0, row]
            value_b = diag[orbital] * b_all[0, row] + (h_b[row] + term_b[orbital])
            a_all[2, row], b_all[1, row] = value, value_b
            put_ends(1, row, value)
            put_ends(1, 16 + row, value_b)

    loop_flat(third)
    loop_flat(fourth)
    for copy in halos[1]:
        copy.wait_recv()
    loop_flat(fifth)
    for copy in halos[2]:
        copy.start()

    def sixth(vector):
        rows = rows_of(vector)
        h_sum, k_sum = interior(lambda bond: [gather(bond, a_all, 2, row) for row in rows], True, True)
        hb_sum, _ = interior(lambda bond: [gather(bond, b_all, 1, row) for row in rows], True, False)
        for orbital, row in enumerate(rows):
            value = 2.0 * (diag[orbital] * a_all[2, row] + h_sum[orbital]) - a_all[1, row]
            value_b = 2.0 * (diag[orbital] * b_all[1, row] + hb_sum[orbital]) - b_all[0, row]
            a_all[3, row], b_all[2, row], c_all[2, row] = value, value_b, k_sum[orbital]

    def seventh(vector):
        rows = rows_of(vector)
        _, k_sum = interior(lambda bond: [gather(bond, a_all, 3, row) for row in rows], False, True)
        hb_sum, _ = interior(lambda bond: [gather(bond, b_all, 2, row) for row in rows], True, False)
        mine = hop(5, [gather_mine(a_all.at[2], row) for row in rows])
        mine_b = hop(5, [gather_mine(b_all.at[1], row) for row in rows])
        for orbital, row in enumerate(rows):
            k_a[row], h_b[row] = k_sum[orbital], hb_sum[orbital]
            tip[row], tip[16 + row] = 2.0 * mine[orbital], 2.0 * mine_b[orbital]

    next_ends(a_all.at[2], a_all.at[1], 0)
    next_ends(b_all.at[1], b_all.at[0], 16)
    for copy in halos[3]:
        copy.start()
    loop(sixth)
    loop(seventh)
    moments_of(0)
    moments_of(1)

    for copy in halos[2]:
        copy.wait_recv()

    def eighth(vector):
        rows = rows_of(vector)
        term = hop(4, [gather_ghost(ghost.at[1], row) for row in rows])
        term_b = hop(4, [gather_ghost(ghost.at[1], 16 + row) for row in rows])
        for orbital, row in enumerate(rows):
            change[row], change[16 + row] = 2.0 * term[orbital], 2.0 * term_b[orbital]
            c_all[2, row] = c_all[2, row] + geo[4, 7] * term[orbital]
            b_all[2, row] = b_all[2, row] + 2.0 * term_b[orbital]

    def ninth(vector):
        rows = rows_of(vector)
        _, k_sum = interior(lambda bond: [gather_ends(bond, row) for row in rows], False, True)
        hb_sum, _ = interior(lambda bond: [gather_ends(bond, 16 + row) for row in rows], True, False)
        for orbital, row in enumerate(rows):
            k_a[row], h_b[row] = k_a[row] + k_sum[orbital], h_b[row] + hb_sum[orbital]

    def tenth(vector):
        term, term_b = ghost_terms(vector, 2)
        for orbital, row in enumerate(rows_of(vector)):
            c_all[3, row] = k_a[row] + geo[4, 7] * term[orbital]
            b_all[3, row] = 2.0 * (diag[orbital] * b_all[2, row] + (h_b[row] + term_b[orbital])) - b_all[1, row]

    loop_flat(eighth)
    loop_flat(ninth)
    moments_of(2)
    for copy, only in zip(early, owns_last):
        pl.when(jnp.logical_not(only))(copy.start)
    for copy in halos[3]:
        copy.wait_recv()
    loop_flat(tenth)
    moments_of(3)

    for copy, only in zip(late_all, owns_last):
        pl.when(only)(copy.start)
    for copy, only in zip(late_one, owns_last):
        pl.when(jnp.logical_not(only))(copy.start)
    mine = tile == NMOM - 1
    for copy in late_all:
        pl.when(mine)(copy.wait_recv)
    for copy in late_one + early:
        pl.when(jnp.logical_not(mine))(copy.wait_recv)
    for m in range(NMOM):
        total = mom[tile, m]
        for other in range(ntile - 1):
            total = total + mom_in[other, m]
        out_ref[m] = total * (-1.0 / VECS)
    for group in halos:
        for copy in group:
            copy.wait_send()
    for copies, when in ((late_all, True), (late_one, False), (early, False)):
        for copy, only in zip(copies, owns_last):
            pl.when(only if when else jnp.logical_not(only))(copy.wait_send)


def body(ndom, ntile, vectors, positions, onsite, neighbors):
    import functools
    rows = NORB * vectors.shape[1]
    hbm = pl.BlockSpec(memory_space=pltpu.HBM)
    tiles = lambda *lead: pltpu.VMEM((*lead, *TILE), F32)
    result = pl.pallas_call(
        functools.partial(kernel, ndom, ntile),
        out_shape=jax.ShapeDtypeStruct((NMOM, *TILE), F32),
        in_specs=[hbm] * 4,
        out_specs=pl.BlockSpec(memory_space=pltpu.VMEM),
        scratch_shapes=[
            pltpu.VMEM(vectors.shape, F32),
            pltpu.VMEM(positions.shape, F32),
            pltpu.VMEM(onsite.shape, F32),
            pltpu.VMEM(neighbors.shape, jnp.int32),
            tiles(3), tiles(8), pltpu.VMEM((5, *TILE), jnp.int32), pltpu.VMEM((6, *TILE), jnp.int32),
            tiles(7, 8), tiles(4, rows), tiles(4, rows), tiles(4, rows),
            tiles(rows), tiles(rows), tiles(rows), tiles(2 * rows), tiles(2 * rows),
            pltpu.VMEM((2, CODE + 1, LANES), F32),
            pltpu.VMEM((3, 2, 2 * rows, LANES), F32),
            pltpu.VMEM((2, CODE + 1, LANES), F32),
            pltpu.VMEM((3, 2, 2 * rows, LANES), F32),
            tiles(NMOM, NMOM), tiles(ntile - 1, NMOM),
            pltpu.SemaphoreType.DMA((4,)),
            pltpu.SemaphoreType.DMA((4, 2)),
            pltpu.SemaphoreType.DMA((4, 2)),
            pltpu.SemaphoreType.DMA((3, ntile - 1)),
            pltpu.SemaphoreType.DMA((3, ntile - 1)),
        ],
        compiler_params=pltpu.CompilerParams(
            collective_id=0, has_side_effects=True, vmem_limit_bytes=16 * 1024 * 1024
        ),
        cost_estimate=pl.CostEstimate(flops=10_000_000, bytes_accessed=150_000, transcendentals=10_000),
    )(*[pltpu.with_memory_space_constraint(x, pltpu.HBM) for x in (vectors, positions, onsite, neighbors)])
    return result.reshape(NMOM, GROUPS * LANES)


def solution(mesh):
    import functools
    in_specs = (P(None, "tile", "dom"), P(None, "dom"), P(None, "dom"), P(None, "dom"))
    out_specs = P("tile", "dom")
    local = functools.partial(body, mesh.shape["dom"], mesh.shape["tile"])
    return jax.shard_map(local, mesh=mesh, in_specs=in_specs, out_specs=out_specs, check_vma=False)
```

```python
import jax
import jax.numpy as jnp
from jax import lax
from jax.experimental import pallas as pl
from jax.experimental.pallas import tpu as pltpu
from jax.sharding import PartitionSpec as P

BND = 128
VECS = 16
NMOM = 4
NORB = 4
LANES = 128
GROUPS = 8

onsite_s = -4.2
onsite_p = 1.72
hop_ss = -2.08
hop_sp = 2.48
hop_pps = 2.72
hop_ppp = -0.72
bond_length = 2.35
energy_scale = 16.0
length_scale = 2.0

MESH = pl.DeviceIdType.MESH
F32 = jnp.float32
TILE = (GROUPS, LANES)
POS, CODE = 16, 19


def lanes_of(source, index):
    return jnp.take_along_axis(source, index, axis=1, mode="promise_in_bounds")


def pick(bits, options):
    for bit in bits:
        options = [jnp.where(bit, options[i + 1], options[i]) for i in range(0, len(options), 2)]
    return options[0]


def kernel(
    ndom, ntile,
    vec_hbm, pos_hbm, ons_hbm, nei_hbm, out_ref,
    vec_in, pos_in, ons_in, nei_in,
    pos, diag, code, low, geo, a_all, b_all, c_all, h_a, h_b, k_a, change, tip,
    send0, send, ghost0, ghost, mom, mom_in,
    in_sem, halo_send, halo_recv, mom_send, mom_recv,
):
    dom, tile = lax.axis_index("dom"), lax.axis_index("tile")
    up, down = lax.rem(dom + 1, ndom), lax.rem(dom + ndom - 1, ndom)

    barrier = pltpu.get_barrier_semaphore()
    for other in (up, down):
        pl.semaphore_signal(barrier, inc=1, device_id={"dom": other}, device_id_type=MESH)
    for step in range(1, ntile):
        peer = lax.rem(tile + step, ntile)
        pl.semaphore_signal(barrier, inc=1, device_id={"tile": peer}, device_id_type=MESH)

    loads = [
        pltpu.make_async_copy(source, target, in_sem.at[i])
        for i, (source, target) in enumerate(
            ((vec_hbm, vec_in), (pos_hbm, pos_in), (nei_hbm, nei_in), (ons_hbm, ons_in))
        )
    ]
    for load in loads:
        load.start()
    for load in loads:
        load.wait()

    for group in range(GROUPS):
        cut = pl.ds(group * LANES, LANES)
        for orbital in range(NORB):
            a_all[0, pl.ds(orbital * 4, 4), group, :] = vec_in[orbital, :, cut]
        pos[:, group, :] = pos_in[:, cut]
        diag[pl.ds(0, 4), group, :] = ons_in[:, cut]
        code[pl.ds(0, 4), group, :] = nei_in[:, cut]
    for orbital in range(NORB):
        base = onsite_s if orbital == 0 else onsite_p
        diag[orbital] = (base + diag[orbital]) / energy_scale
    for side, group in ((0, 0), (1, GROUPS - 1)):
        cut = pl.ds(group * LANES, LANES)
        for orbital in range(NORB):
            send0[side, pl.ds(orbital * 4, 4), :] = vec_in[orbital, :, cut]
        send0[side, pl.ds(POS, 3), :] = pos_in[:, cut]
        send0[side, pl.ds(CODE, 1), :] = nei_in[0:1, cut].astype(F32)

    def both_ways(sources, target, send_sem, recv_sem):
        return [
            pltpu.make_async_remote_copy(
                src_ref=sources[side], dst_ref=target.at[1 - side],
                send_sem=send_sem.at[side], recv_sem=recv_sem.at[1 - side],
                device_id={"dom": other}, device_id_type=MESH,
            )
            for side, other in ((0, down), (1, up))
        ]

    halos = [both_ways((send0.at[0], send0.at[1]), ghost0, halo_send.at[0], halo_recv.at[0])] + [
        both_ways((send.at[i, 0], send.at[i, 1]), ghost.at[i], halo_send.at[i + 1], halo_recv.at[i + 1])
        for i in range(3)
    ]

    for bond in range(4):
        low[bond] = jnp.bitwise_and(code[bond], LANES - 1)
        code[bond] = lax.shift_right_logical(code[bond], 7) - 1

    def gather(bond, ref, *row):
        bits = [jnp.bitwise_and(code[bond], 1 << bit) != 0 for bit in range(3)]
        return pick(bits, [
            lanes_of(jnp.broadcast_to(ref[(*row, pl.ds(group, 1), slice(None))], TILE), low[bond])
            for group in range(GROUPS)
        ])

    upper_half = lax.broadcasted_iota(jnp.int32, TILE, 0) >= GROUPS // 2

    def halves(below, above):
        return jnp.where(upper_half, jnp.broadcast_to(above, TILE), jnp.broadcast_to(below, TILE))

    def ends_of(ref, row):
        return halves(ref[0, pl.ds(row, 1), :], ref[1, pl.ds(row, 1), :])

    def gather_ghost(ref, row):
        return lanes_of(ends_of(ref, row), low[0])

    def put_geometry(slot, center, partner, bonded):
        offset = [partner[axis] - center[axis] for axis in range(3)]
        distance = jnp.sqrt(offset[0] * offset[0] + offset[1] * offset[1] + offset[2] * offset[2])
        away = distance - bond_length
        radial = jnp.where(bonded, jnp.exp(-0.5 * away * away) / energy_scale, 0.0)
        inverse = 1.0 / jnp.maximum(distance, 1.0)
        geo[slot, 0] = hop_ss * radial
        geo[slot, 1] = hop_sp * radial
        geo[slot, 2] = (hop_pps - hop_ppp) * radial
        geo[slot, 3] = hop_ppp * radial
        for axis in range(3):
            geo[slot, 4 + axis] = offset[axis] * inverse
        geo[slot, 7] = offset[0] * (-1.0 / length_scale)

    def hop(slot, beside):
        along = geo[slot, 4] * beside[1] + geo[slot, 5] * beside[2] + geo[slot, 6] * beside[3]
        mixed = geo[slot, 2] * along - geo[slot, 1] * beside[0]
        result = [geo[slot, 0] * beside[0] + geo[slot, 1] * along]
        for axis in range(3):
            result.append(geo[slot, 4 + axis] * mixed + geo[slot, 3] * beside[1 + axis])
        return result

    own_pos = [pos[axis] for axis in range(3)]
    for bond in range(4):
        inside = jnp.logical_and(code[bond] >= 0, code[bond] < GROUPS)
        put_geometry(bond, own_pos, [gather(bond, pos, axis) for axis in range(3)], inside)

    def put_own_ends():
        for side, group in ((0, 0), (1, GROUPS - 1)):
            for bond in range(4):
                place = pl.ds(side * 4 + bond, 1)
                low[5, place, :] = low[bond, pl.ds(group, 1), :]
                code[4, place, :] = code[bond, pl.ds(group, 1), :]
                for entry in range(7):
                    geo[6, entry, place, :] = geo[bond, entry, pl.ds(group, 1), :]
        for orbital in range(NORB):
            diag[4 + orbital] = halves(diag[orbital, pl.ds(0, 1), :], diag[orbital, pl.ds(GROUPS - 1, 1), :])

    def bond_sum(value):
        value = value + pltpu.roll(value, 1, 0)
        return value + pltpu.roll(value, 2, 0)

    def own_ends(ref, row):
        return halves(ref[row, pl.ds(0, 1), :], ref[row, pl.ds(GROUPS - 1, 1), :])

    def next_ends(current, past, row_shift):
        bits = [jnp.bitwise_and(code[4], 1 << bit) != 0 for bit in range(3)]
        for vector in range(4):
            rows = rows_of(vector)
            term = hop(6, [
                pick(bits, [
                    lanes_of(jnp.broadcast_to(current[row, pl.ds(group, 1), :], TILE), low[5])
                    for group in range(GROUPS)
                ])
                for row in rows
            ])
            for orbital, row in enumerate(rows):
                value = diag[4 + orbital] * own_ends(current, row) + bond_sum(term[orbital])
                value = 2.0 * value - own_ends(past, row)
                send[2, 0, pl.ds(row_shift + row, 1), :] = value[3:4]
                send[2, 1, pl.ds(row_shift + row, 1), :] = value[7:8]

    def rows_of(vector):
        return [orbital * 4 + vector for orbital in range(NORB)]

    def add(total, term):
        return term if total is None else [x + y for x, y in zip(total, term)]

    def put_ends(slot, row, value):
        send[slot, 0, pl.ds(row, 1), :] = value[0:1]
        send[slot, 1, pl.ds(row, 1), :] = value[GROUPS - 1:]

    def interior(found, want_h, want_k):
        h_sum = k_sum = None
        for bond in range(4):
            term = hop(bond, found(bond))
            if want_h:
                h_sum = add(h_sum, term)
            if want_k:
                drift = geo[bond, 7]
                k_sum = add(k_sum, [drift * x for x in term])
        return h_sum, k_sum

    def ends_at(bond, first, last):
        group, index = code[bond], low[bond]
        first = lanes_of(jnp.broadcast_to(first, TILE), index)
        last = lanes_of(jnp.broadcast_to(last, TILE), index)
        return jnp.where(group == 0, first, jnp.where(group == GROUPS - 1, last, 0.0))

    def gather_ends(bond, row):
        return ends_at(bond, change[row, pl.ds(0, 1), :], change[row, pl.ds(GROUPS - 1, 1), :])

    def gather_mine(ref, row):
        return lanes_of(halves(ref[row, pl.ds(0, 1), :], ref[row, pl.ds(GROUPS - 1, 1), :]), low[4])

    def loop(function):
        lax.fori_loop(0, 4, lambda vector, carry: function(vector) or carry, 0)

    def loop_flat(function):
        for vector in range(4):
            function(vector)

    def moments_of(step):
        pairs = [(step, m) for m in range(step + 1)] + [(n, step) for n in range(step)]

        def moments(row, sums):
            b_rows = [b_all[n, row] for n in range(step + 1)]
            c_rows = [c_all[m, row] if m else b_rows[0] for m in range(step + 1)]
            return tuple(total + b_rows[n] * c_rows[m] for total, (n, m) in zip(sums, pairs))

        sums = lax.fori_loop(0, 16, moments, tuple(jnp.zeros(TILE, F32) for _ in pairs), unroll=4)
        for (n, m), total in zip(pairs, sums):
            mom[n, m] = total

    def to_peer(step, part, rows):
        peer = lax.rem(tile + step, ntile)
        return pltpu.make_async_remote_copy(
            src_ref=mom.at[peer, rows], dst_ref=mom_in.at[step - 1, rows],
            send_sem=mom_send.at[part, step - 1], recv_sem=mom_recv.at[part, step - 1],
            device_id={"tile": peer}, device_id_type=MESH,
        )

    others = sorted(range(1, ntile), key=lambda step: -min(step, ntile - step))
    owns_last = [lax.rem(tile + step, ntile) == NMOM - 1 for step in others]
    early = [to_peer(step, 0, pl.ds(0, NMOM - 1)) for step in others]
    late_one = [to_peer(step, 1, pl.ds(NMOM - 1, 1)) for step in others]
    late_all = [to_peer(step, 2, pl.ds(0, NMOM)) for step in others]

    def first(vector):
        rows = rows_of(vector)
        h_sum, k_sum = interior(lambda bond: [gather(bond, a_all, 0, row) for row in rows], True, True)
        for orbital, row in enumerate(rows):
            value = diag[orbital] * a_all[0, row] + h_sum[orbital]
            a_all[1, row] = value
            b_all[0, row] = k_sum[orbital]
            put_ends(0, row, value)
            put_ends(0, 16 + row, k_sum[orbital])

    def second(vector):
        rows = rows_of(vector)
        h_sum, k_sum = interior(lambda bond: [gather(bond, a_all, 1, row) for row in rows], True, True)
        hb_sum, _ = interior(lambda bond: [gather(bond, b_all, 0, row) for row in rows], True, False)
        for orbital, row in enumerate(rows):
            h_a[row], k_a[row], h_b[row] = h_sum[orbital], k_sum[orbital], hb_sum[orbital]

    loop(first)
    pl.semaphore_wait(barrier, 2 + ntile - 1)
    for copy in halos[0] + halos[1]:
        copy.start()
    loop(second)
    put_own_ends()

    for copy in halos[0]:
        copy.wait_recv()
    outside = jnp.logical_or(code[0] == -1, code[0] == GROUPS)
    put_geometry(4, own_pos, [gather_ghost(ghost0, POS + axis) for axis in range(3)], outside)
    number = ends_of(ghost0, CODE).astype(jnp.int32)
    group = lax.shift_right_logical(number, 7) - 1
    low[4] = jnp.bitwise_and(number, LANES - 1)
    put_geometry(
        5, [ends_of(ghost0, POS + axis) for axis in range(3)], [gather_mine(pos, axis) for axis in range(3)],
        jnp.logical_or(group == -1, group == GROUPS),
    )

    def third(vector):
        rows = rows_of(vector)
        term = hop(4, [gather_ghost(ghost0, row) for row in rows])
        mine = hop(5, [gather_mine(a_all.at[0], row) for row in rows])
        for orbital, row in enumerate(rows):
            moved = geo[4, 7] * term[orbital]
            change[row] = term[orbital]
            a_all[1, row] = a_all[1, row] + term[orbital]
            b_all[0, row] = b_all[0, row] + moved
            tip[row], tip[16 + row] = mine[orbital], geo[5, 7] * mine[orbital]

    def fourth():
        for bond in range(4):
            drift = geo[bond, 7]
            moved = ends_at(bond, geo[4, 7, pl.ds(0, 1), :], geo[4, 7, pl.ds(GROUPS - 1, 1), :])
            for vector in range(4):
                rows = rows_of(vector)
                term = hop(bond, [gather_ends(bond, row) for row in rows])
                for orbital, row in enumerate(rows):
                    h_a[row] = h_a[row] + term[orbital]
                    k_a[row] = k_a[row] + drift * term[orbital]
                    h_b[row] = h_b[row] + moved * term[orbital]

    def ghost_terms(vector, slot):
        rows = rows_of(vector)
        return [
            hop(4, [lanes_of(tip[shift + row] + ends_of(ghost.at[slot], shift + row), low[0]) for row in rows])
            for shift in (0, 16)
        ]

    def fifth(vector):
        term, term_b = ghost_terms(vector, 0)
        for orbital, row in enumerate(rows_of(vector)):
            c_all[1, row] = k_a[row] + geo[4, 7] * term[orbital]
            value = 2.0 * (diag[orbital] * a_all[1, row] + (h_a[row] + term[orbital])) - a_all[0, row]
            value_b = diag[orbital] * b_all[0, row] + (h_b[row] + term_b[orbital])
            a_all[2, row], b_all[1, row] = value, value_b
            put_ends(1, row, value)
            put_ends(1, 16 + row, value_b)

    loop_flat(third)
    fourth()
    for copy in halos[1]:
        copy.wait_recv()
    loop_flat(fifth)
    for copy in halos[2][::-1]:
        copy.start()

    def sixth(vector):
        rows = rows_of(vector)
        h_sum, k_sum = interior(lambda bond: [gather(bond, a_all, 2, row) for row in rows], True, True)
        hb_sum, _ = interior(lambda bond: [gather(bond, b_all, 1, row) for row in rows], True, False)
        for orbital, row in enumerate(rows):
            value = 2.0 * (diag[orbital] * a_all[2, row] + h_sum[orbital]) - a_all[1, row]
            value_b = 2.0 * (diag[orbital] * b_all[1, row] + hb_sum[orbital]) - b_all[0, row]
            a_all[3, row], b_all[2, row], c_all[2, row] = value, value_b, k_sum[orbital]

    def seventh(vector):
        rows = rows_of(vector)
        _, k_sum = interior(lambda bond: [gather(bond, a_all, 3, row) for row in rows], False, True)
        hb_sum, _ = interior(lambda bond: [gather(bond, b_all, 2, row) for row in rows], True, False)
        mine = hop(5, [gather_mine(a_all.at[2], row) for row in rows])
        mine_b = hop(5, [gather_mine(b_all.at[1], row) for row in rows])
        for orbital, row in enumerate(rows):
            k_a[row], h_b[row] = k_sum[orbital], hb_sum[orbital]
            tip[row], tip[16 + row] = 2.0 * mine[orbital], 2.0 * mine_b[orbital]

    next_ends(a_all.at[2], a_all.at[1], 0)
    next_ends(b_all.at[1], b_all.at[0], 16)
    for copy in halos[3][::-1]:
        copy.start()
    loop(sixth)
    loop(seventh)
    moments_of(0)
    moments_of(1)

    for copy in halos[2]:
        copy.wait_recv()

    def eighth(vector):
        rows = rows_of(vector)
        term = hop(4, [gather_ghost(ghost.at[1], row) for row in rows])
        term_b = hop(4, [gather_ghost(ghost.at[1], 16 + row) for row in rows])
        for orbital, row in enumerate(rows):
            change[row], change[16 + row] = 2.0 * term[orbital], 2.0 * term_b[orbital]
            c_all[2, row] = c_all[2, row] + geo[4, 7] * term[orbital]
            b_all[2, row] = b_all[2, row] + 2.0 * term_b[orbital]

    def ninth(vector):
        rows = rows_of(vector)
        _, k_sum = interior(lambda bond: [gather_ends(bond, row) for row in rows], False, True)
        hb_sum, _ = interior(lambda bond: [gather_ends(bond, 16 + row) for row in rows], True, False)
        for orbital, row in enumerate(rows):
            k_a[row], h_b[row] = k_a[row] + k_sum[orbital], h_b[row] + hb_sum[orbital]

    last_pairs = [(3, m) for m in range(4)] + [(n, 3) for n in range(3)]

    def tenth():
        sums = [None] * len(last_pairs)
        for vector in range(4):
            term, term_b = ghost_terms(vector, 2)
            for orbital, row in enumerate(rows_of(vector)):
                c_last = k_a[row] + geo[4, 7] * term[orbital]
                b_last = 2.0 * (diag[orbital] * b_all[2, row] + (h_b[row] + term_b[orbital])) - b_all[1, row]
                b_rows = [b_all[n, row] for n in range(3)] + [b_last]
                c_rows = [b_rows[0], c_all[1, row], c_all[2, row], c_last]
                for at, (n, m) in enumerate(last_pairs):
                    part = b_rows[n] * c_rows[m]
                    sums[at] = part if sums[at] is None else sums[at] + part
        for (n, m), total in zip(last_pairs, sums):
            mom[n, m] = total

    loop_flat(eighth)
    loop_flat(ninth)
    moments_of(2)
    for copy, only in zip(early, owns_last):
        pl.when(jnp.logical_not(only))(copy.start)
    for copy in halos[3]:
        copy.wait_recv()
    tenth()

    for copy, only in zip(late_all, owns_last):
        pl.when(only)(copy.start)
    for copy, only in zip(late_one, owns_last):
        pl.when(jnp.logical_not(only))(copy.start)
    mine = tile == NMOM - 1
    for copy in late_all:
        pl.when(mine)(copy.wait_recv)
    for copy in late_one + early:
        pl.when(jnp.logical_not(mine))(copy.wait_recv)
    for m in range(NMOM):
        total = mom[tile, m]
        for other in range(ntile - 1):
            total = total + mom_in[other, m]
        out_ref[m] = total * (-1.0 / VECS)
    for group in halos:
        for copy in group:
            copy.wait_send()
    for copies, when in ((late_all, True), (late_one, False), (early, False)):
        for copy, only in zip(copies, owns_last):
            pl.when(only if when else jnp.logical_not(only))(copy.wait_send)


def body(ndom, ntile, vectors, positions, onsite, neighbors):
    import functools
    rows = NORB * vectors.shape[1]
    hbm = pl.BlockSpec(memory_space=pltpu.HBM)
    tiles = lambda *lead: pltpu.VMEM((*lead, *TILE), F32)
    result = pl.pallas_call(
        functools.partial(kernel, ndom, ntile),
        out_shape=jax.ShapeDtypeStruct((NMOM, *TILE), F32),
        in_specs=[hbm] * 4,
        out_specs=pl.BlockSpec(memory_space=pltpu.VMEM),
        scratch_shapes=[
            pltpu.VMEM(vectors.shape, F32),
            pltpu.VMEM(positions.shape, F32),
            pltpu.VMEM(onsite.shape, F32),
            pltpu.VMEM(neighbors.shape, jnp.int32),
            tiles(3), tiles(8), pltpu.VMEM((5, *TILE), jnp.int32), pltpu.VMEM((6, *TILE), jnp.int32),
            tiles(7, 8), tiles(4, rows), tiles(4, rows), tiles(4, rows),
            tiles(rows), tiles(rows), tiles(rows), tiles(2 * rows), tiles(2 * rows),
            pltpu.VMEM((2, CODE + 1, LANES), F32),
            pltpu.VMEM((3, 2, 2 * rows, LANES), F32),
            pltpu.VMEM((2, CODE + 1, LANES), F32),
            pltpu.VMEM((3, 2, 2 * rows, LANES), F32),
            tiles(NMOM, NMOM), tiles(ntile - 1, NMOM),
            pltpu.SemaphoreType.DMA((4,)),
            pltpu.SemaphoreType.DMA((4, 2)),
            pltpu.SemaphoreType.DMA((4, 2)),
            pltpu.SemaphoreType.DMA((3, ntile - 1)),
            pltpu.SemaphoreType.DMA((3, ntile - 1)),
        ],
        compiler_params=pltpu.CompilerParams(
            collective_id=0, has_side_effects=True, vmem_limit_bytes=16 * 1024 * 1024
        ),
        cost_estimate=pl.CostEstimate(flops=10_000_000, bytes_accessed=150_000, transcendentals=10_000),
    )(*[pltpu.with_memory_space_constraint(x, pltpu.HBM) for x in (vectors, positions, onsite, neighbors)])
    return result.reshape(NMOM, GROUPS * LANES)


def solution(mesh):
    import functools
    in_specs = (P(None, "tile", "dom"), P(None, "dom"), P(None, "dom"), P(None, "dom"))
    out_specs = P("tile", "dom")
    local = functools.partial(body, mesh.shape["dom"], mesh.shape["tile"])
    return jax.shard_map(local, mesh=mesh, in_specs=in_specs, out_specs=out_specs, check_vma=False)
```

```python
import jax
import jax.numpy as jnp
from jax import lax
from jax.experimental import pallas as pl
from jax.experimental.pallas import tpu as pltpu
from jax.sharding import PartitionSpec as P

BND = 128
VECS = 16
NMOM = 4
NORB = 4
LANES = 128
GROUPS = 8

onsite_s = -4.2
onsite_p = 1.72
hop_ss = -2.08
hop_sp = 2.48
hop_pps = 2.72
hop_ppp = -0.72
bond_length = 2.35
energy_scale = 16.0
length_scale = 2.0

MESH = pl.DeviceIdType.MESH
F32 = jnp.float32
TILE = (GROUPS, LANES)
POS, CODE = 16, 19


def lanes_of(source, index):
    return jnp.take_along_axis(source, index, axis=1, mode="promise_in_bounds")


def pick(bits, options):
    for bit in bits:
        options = [jnp.where(bit, options[i + 1], options[i]) for i in range(0, len(options), 2)]
    return options[0]


def kernel(
    ndom, ntile,
    vec_hbm, pos_hbm, ons_hbm, nei_hbm, out_ref,
    vec_in, pos_in, ons_in, nei_in,
    pos, diag, code, low, geo, a_all, b_all, c_all, h_a, h_b, k_a, change, tip,
    send0, send, ghost0, ghost, mom, mom_in,
    in_sem, halo_send, halo_recv, mom_send, mom_recv,
):
    dom, tile = lax.axis_index("dom"), lax.axis_index("tile")
    up, down = lax.rem(dom + 1, ndom), lax.rem(dom + ndom - 1, ndom)

    barrier = pltpu.get_barrier_semaphore()
    for other in (up, down):
        pl.semaphore_signal(barrier, inc=1, device_id={"dom": other}, device_id_type=MESH)
    for step in range(1, ntile):
        peer = lax.rem(tile + step, ntile)
        pl.semaphore_signal(barrier, inc=1, device_id={"tile": peer}, device_id_type=MESH)

    loads = [
        pltpu.make_async_copy(source, target, in_sem.at[i])
        for i, (source, target) in enumerate(
            ((vec_hbm, vec_in), (pos_hbm, pos_in), (nei_hbm, nei_in), (ons_hbm, ons_in))
        )
    ]
    for load in loads:
        load.start()
    for load in loads:
        load.wait()

    for group in range(GROUPS):
        cut = pl.ds(group * LANES, LANES)
        for orbital in range(NORB):
            a_all[0, pl.ds(orbital * 4, 4), group, :] = vec_in[orbital, :, cut]
        pos[:, group, :] = pos_in[:, cut]
        diag[pl.ds(0, 4), group, :] = ons_in[:, cut]
        code[pl.ds(0, 4), group, :] = nei_in[:, cut]
    for orbital in range(NORB):
        base = onsite_s if orbital == 0 else onsite_p
        diag[orbital] = (base + diag[orbital]) / energy_scale
    for side, group in ((0, 0), (1, GROUPS - 1)):
        cut = pl.ds(group * LANES, LANES)
        for orbital in range(NORB):
            send0[side, pl.ds(orbital * 4, 4), :] = vec_in[orbital, :, cut]
        send0[side, pl.ds(POS, 3), :] = pos_in[:, cut]
        send0[side, pl.ds(CODE, 1), :] = nei_in[0:1, cut].astype(F32)

    def both_ways(sources, target, send_sem, recv_sem):
        return [
            pltpu.make_async_remote_copy(
                src_ref=sources[side], dst_ref=target.at[1 - side],
                send_sem=send_sem.at[side], recv_sem=recv_sem.at[1 - side],
                device_id={"dom": other}, device_id_type=MESH,
            )
            for side, other in ((0, down), (1, up))
        ]

    halos = [both_ways((send0.at[0], send0.at[1]), ghost0, halo_send.at[0], halo_recv.at[0])] + [
        both_ways((send.at[i, 0], send.at[i, 1]), ghost.at[i], halo_send.at[i + 1], halo_recv.at[i + 1])
        for i in range(3)
    ]

    for bond in range(4):
        low[bond] = jnp.bitwise_and(code[bond], LANES - 1)
        code[bond] = lax.shift_right_logical(code[bond], 7) - 1

    def gather(bond, ref, *row):
        bits = [jnp.bitwise_and(code[bond], 1 << bit) != 0 for bit in range(3)]
        return pick(bits, [
            lanes_of(jnp.broadcast_to(ref[(*row, pl.ds(group, 1), slice(None))], TILE), low[bond])
            for group in range(GROUPS)
        ])

    upper_half = lax.broadcasted_iota(jnp.int32, TILE, 0) >= GROUPS // 2

    def halves(below, above):
        return jnp.where(upper_half, jnp.broadcast_to(above, TILE), jnp.broadcast_to(below, TILE))

    def ends_of(ref, row):
        return halves(ref[0, pl.ds(row, 1), :], ref[1, pl.ds(row, 1), :])

    def gather_ghost(ref, row):
        return lanes_of(ends_of(ref, row), low[0])

    def put_geometry(slot, center, partner, bonded):
        offset = [partner[axis] - center[axis] for axis in range(3)]
        distance = jnp.sqrt(offset[0] * offset[0] + offset[1] * offset[1] + offset[2] * offset[2])
        away = distance - bond_length
        radial = jnp.where(bonded, jnp.exp(-0.5 * away * away) / energy_scale, 0.0)
        inverse = 1.0 / jnp.maximum(distance, 1.0)
        geo[slot, 0] = hop_ss * radial
        geo[slot, 1] = hop_sp * radial
        geo[slot, 2] = (hop_pps - hop_ppp) * radial
        geo[slot, 3] = hop_ppp * radial
        for axis in range(3):
            geo[slot, 4 + axis] = offset[axis] * inverse
        geo[slot, 7] = offset[0] * (-1.0 / length_scale)

    def hop(slot, beside):
        along = geo[slot, 4] * beside[1] + geo[slot, 5] * beside[2] + geo[slot, 6] * beside[3]
        mixed = geo[slot, 2] * along - geo[slot, 1] * beside[0]
        result = [geo[slot, 0] * beside[0] + geo[slot, 1] * along]
        for axis in range(3):
            result.append(geo[slot, 4 + axis] * mixed + geo[slot, 3] * beside[1 + axis])
        return result

    own_pos = [pos[axis] for axis in range(3)]
    for bond in range(4):
        inside = jnp.logical_and(code[bond] >= 0, code[bond] < GROUPS)
        put_geometry(bond, own_pos, [gather(bond, pos, axis) for axis in range(3)], inside)

    def put_own_ends():
        for side, group in ((0, 0), (1, GROUPS - 1)):
            for bond in range(4):
                place = pl.ds(side * 4 + bond, 1)
                low[5, place, :] = low[bond, pl.ds(group, 1), :]
                code[4, place, :] = code[bond, pl.ds(group, 1), :]
                for entry in range(7):
                    geo[6, entry, place, :] = geo[bond, entry, pl.ds(group, 1), :]
        for orbital in range(NORB):
            diag[4 + orbital] = halves(diag[orbital, pl.ds(0, 1), :], diag[orbital, pl.ds(GROUPS - 1, 1), :])

    def bond_sum(value):
        value = value + pltpu.roll(value, 1, 0)
        return value + pltpu.roll(value, 2, 0)

    def own_ends(ref, row):
        return halves(ref[row, pl.ds(0, 1), :], ref[row, pl.ds(GROUPS - 1, 1), :])

    def next_ends(current, past, row_shift):
        bits = [jnp.bitwise_and(code[4], 1 << bit) != 0 for bit in range(3)]
        for vector in range(4):
            rows = rows_of(vector)
            term = hop(6, [
                pick(bits, [
                    lanes_of(jnp.broadcast_to(current[row, pl.ds(group, 1), :], TILE), low[5])
                    for group in range(GROUPS)
                ])
                for row in rows
            ])
            for orbital, row in enumerate(rows):
                value = diag[4 + orbital] * own_ends(current, row) + bond_sum(term[orbital])
                value = 2.0 * value - own_ends(past, row)
                send[2, 0, pl.ds(row_shift + row, 1), :] = value[3:4]
                send[2, 1, pl.ds(row_shift + row, 1), :] = value[7:8]

    def rows_of(vector):
        return [orbital * 4 + vector for orbital in range(NORB)]

    def add(total, term):
        return term if total is None else [x + y for x, y in zip(total, term)]

    def put_ends(slot, row, value):
        send[slot, 0, pl.ds(row, 1), :] = value[0:1]
        send[slot, 1, pl.ds(row, 1), :] = value[GROUPS - 1:]

    def interior(found, want_h, want_k):
        h_sum = k_sum = None
        for bond in range(4):
            term = hop(bond, found(bond))
            if want_h:
                h_sum = add(h_sum, term)
            if want_k:
                drift = geo[bond, 7]
                k_sum = add(k_sum, [drift * x for x in term])
        return h_sum, k_sum

    def ends_at(bond, first, last):
        group, index = code[bond], low[bond]
        first = lanes_of(jnp.broadcast_to(first, TILE), index)
        last = lanes_of(jnp.broadcast_to(last, TILE), index)
        return jnp.where(group == 0, first, jnp.where(group == GROUPS - 1, last, 0.0))

    def gather_ends(bond, row):
        return ends_at(bond, change[row, pl.ds(0, 1), :], change[row, pl.ds(GROUPS - 1, 1), :])

    def gather_mine(ref, row):
        return lanes_of(halves(ref[row, pl.ds(0, 1), :], ref[row, pl.ds(GROUPS - 1, 1), :]), low[4])

    def loop(function):
        lax.fori_loop(0, 4, lambda vector, carry: function(vector) or carry, 0)

    def loop_flat(function):
        for vector in range(4):
            function(vector)

    def moments_of(step):
        pairs = [(step, m) for m in range(step + 1)] + [(n, step) for n in range(step)]

        def moments(row, sums):
            b_rows = [b_all[n, row] for n in range(step + 1)]
            c_rows = [c_all[m, row] if m else b_rows[0] for m in range(step + 1)]
            return tuple(total + b_rows[n] * c_rows[m] for total, (n, m) in zip(sums, pairs))

        sums = lax.fori_loop(0, 16, moments, tuple(jnp.zeros(TILE, F32) for _ in pairs), unroll=4)
        for (n, m), total in zip(pairs, sums):
            mom[n, m] = total

    def to_peer(step):
        peer = lax.rem(tile + step, ntile)
        return pltpu.make_async_remote_copy(
            src_ref=mom.at[peer], dst_ref=mom_in.at[step - 1],
            send_sem=mom_send.at[step - 1], recv_sem=mom_recv.at[step - 1],
            device_id={"tile": peer}, device_id_type=MESH,
        )

    others = sorted(range(1, ntile), key=lambda step: -min(step, ntile - step))
    to_owners = [to_peer(step) for step in others]

    def first(vector):
        rows = rows_of(vector)
        h_sum, k_sum = interior(lambda bond: [gather(bond, a_all, 0, row) for row in rows], True, True)
        for orbital, row in enumerate(rows):
            value = diag[orbital] * a_all[0, row] + h_sum[orbital]
            a_all[1, row] = value
            b_all[0, row] = k_sum[orbital]
            put_ends(0, row, value)
            put_ends(0, 16 + row, k_sum[orbital])

    def second(vector):
        rows = rows_of(vector)
        h_sum, k_sum = interior(lambda bond: [gather(bond, a_all, 1, row) for row in rows], True, True)
        hb_sum, _ = interior(lambda bond: [gather(bond, b_all, 0, row) for row in rows], True, False)
        for orbital, row in enumerate(rows):
            h_a[row], k_a[row], h_b[row] = h_sum[orbital], k_sum[orbital], hb_sum[orbital]

    loop(first)
    pl.semaphore_wait(barrier, 2 + ntile - 1)
    for copy in halos[0] + halos[1]:
        copy.start()
    loop(second)
    put_own_ends()

    for copy in halos[0]:
        copy.wait_recv()
    outside = jnp.logical_or(code[0] == -1, code[0] == GROUPS)
    put_geometry(4, own_pos, [gather_ghost(ghost0, POS + axis) for axis in range(3)], outside)
    number = ends_of(ghost0, CODE).astype(jnp.int32)
    group = lax.shift_right_logical(number, 7) - 1
    low[4] = jnp.bitwise_and(number, LANES - 1)
    put_geometry(
        5, [ends_of(ghost0, POS + axis) for axis in range(3)], [gather_mine(pos, axis) for axis in range(3)],
        jnp.logical_or(group == -1, group == GROUPS),
    )

    def third(vector):
        rows = rows_of(vector)
        term = hop(4, [gather_ghost(ghost0, row) for row in rows])
        mine = hop(5, [gather_mine(a_all.at[0], row) for row in rows])
        for orbital, row in enumerate(rows):
            moved = geo[4, 7] * term[orbital]
            change[row] = term[orbital]
            a_all[1, row] = a_all[1, row] + term[orbital]
            b_all[0, row] = b_all[0, row] + moved
            tip[row], tip[16 + row] = mine[orbital], geo[5, 7] * mine[orbital]

    def fourth():
        for bond in range(4):
            drift = geo[bond, 7]
            moved = ends_at(bond, geo[4, 7, pl.ds(0, 1), :], geo[4, 7, pl.ds(GROUPS - 1, 1), :])
            for vector in range(4):
                rows = rows_of(vector)
                term = hop(bond, [gather_ends(bond, row) for row in rows])
                for orbital, row in enumerate(rows):
                    h_a[row] = h_a[row] + term[orbital]
                    k_a[row] = k_a[row] + drift * term[orbital]
                    h_b[row] = h_b[row] + moved * term[orbital]

    def ghost_terms(vector, slot):
        rows = rows_of(vector)
        return [
            hop(4, [lanes_of(tip[shift + row] + ends_of(ghost.at[slot], shift + row), low[0]) for row in rows])
            for shift in (0, 16)
        ]

    def fifth(vector):
        term, term_b = ghost_terms(vector, 0)
        for orbital, row in enumerate(rows_of(vector)):
            c_all[1, row] = k_a[row] + geo[4, 7] * term[orbital]
            value = 2.0 * (diag[orbital] * a_all[1, row] + (h_a[row] + term[orbital])) - a_all[0, row]
            value_b = diag[orbital] * b_all[0, row] + (h_b[row] + term_b[orbital])
            a_all[2, row], b_all[1, row] = value, value_b
            put_ends(1, row, value)
            put_ends(1, 16 + row, value_b)

    loop_flat(third)
    fourth()
    for copy in halos[1]:
        copy.wait_recv()
    loop_flat(fifth)
    for copy in halos[2][::-1]:
        copy.start()

    def sixth(vector):
        rows = rows_of(vector)
        h_sum, k_sum = interior(lambda bond: [gather(bond, a_all, 2, row) for row in rows], True, True)
        hb_sum, _ = interior(lambda bond: [gather(bond, b_all, 1, row) for row in rows], True, False)
        for orbital, row in enumerate(rows):
            value = 2.0 * (diag[orbital] * a_all[2, row] + h_sum[orbital]) - a_all[1, row]
            value_b = 2.0 * (diag[orbital] * b_all[1, row] + hb_sum[orbital]) - b_all[0, row]
            a_all[3, row], b_all[2, row], c_all[2, row] = value, value_b, k_sum[orbital]

    def seventh(vector):
        rows = rows_of(vector)
        _, k_sum = interior(lambda bond: [gather(bond, a_all, 3, row) for row in rows], False, True)
        hb_sum, _ = interior(lambda bond: [gather(bond, b_all, 2, row) for row in rows], True, False)
        mine = hop(5, [gather_mine(a_all.at[2], row) for row in rows])
        mine_b = hop(5, [gather_mine(b_all.at[1], row) for row in rows])
        for orbital, row in enumerate(rows):
            k_a[row], h_b[row] = k_sum[orbital], hb_sum[orbital]
            tip[row], tip[16 + row] = 2.0 * mine[orbital], 2.0 * mine_b[orbital]

    next_ends(a_all.at[2], a_all.at[1], 0)
    next_ends(b_all.at[1], b_all.at[0], 16)
    for copy in halos[3][::-1]:
        copy.start()
    loop(sixth)
    loop(seventh)
    moments_of(0)
    moments_of(1)

    for copy in halos[2]:
        copy.wait_recv()

    middle_pairs = [(2, m) for m in range(3)] + [(n, 2) for n in range(2)]

    def eighth():
        sums = [None] * len(middle_pairs)
        for vector in range(4):
            rows = rows_of(vector)
            term = hop(4, [gather_ghost(ghost.at[1], row) for row in rows])
            term_b = hop(4, [gather_ghost(ghost.at[1], 16 + row) for row in rows])
            for orbital, row in enumerate(rows):
                change_a, change_b = 2.0 * term[orbital], 2.0 * term_b[orbital]
                change[row], change[16 + row] = change_a, change_b
                c_two = c_all[2, row] + geo[4, 7] * term[orbital]
                b_two = b_all[2, row] + change_b
                c_all[2, row], b_all[2, row] = c_two, b_two
                b_rows = [b_all[0, row], b_all[1, row], b_two]
                c_rows = [b_rows[0], c_all[1, row], c_two]
                for at, (n, m) in enumerate(middle_pairs):
                    part = b_rows[n] * c_rows[m]
                    sums[at] = part if sums[at] is None else sums[at] + part
        for (n, m), total in zip(middle_pairs, sums):
            mom[n, m] = total

    def ninth(vector):
        rows = rows_of(vector)
        _, k_sum = interior(lambda bond: [gather_ends(bond, row) for row in rows], False, True)
        hb_sum, _ = interior(lambda bond: [gather_ends(bond, 16 + row) for row in rows], True, False)
        for orbital, row in enumerate(rows):
            k_a[row], h_b[row] = k_a[row] + k_sum[orbital], h_b[row] + hb_sum[orbital]

    last_pairs = [(3, m) for m in range(4)] + [(n, 3) for n in range(3)]

    def tenth():
        sums = [None] * len(last_pairs)
        for vector in range(4):
            term, term_b = ghost_terms(vector, 2)
            for orbital, row in enumerate(rows_of(vector)):
                c_last = k_a[row] + geo[4, 7] * term[orbital]
                b_last = 2.0 * (diag[orbital] * b_all[2, row] + (h_b[row] + term_b[orbital])) - b_all[1, row]
                b_rows = [b_all[n, row] for n in range(3)] + [b_last]
                c_rows = [b_rows[0], c_all[1, row], c_all[2, row], c_last]
                for at, (n, m) in enumerate(last_pairs):
                    part = b_rows[n] * c_rows[m]
                    sums[at] = part if sums[at] is None else sums[at] + part
        for (n, m), total in zip(last_pairs, sums):
            mom[n, m] = total

    eighth()
    loop_flat(ninth)
    for copy in halos[3]:
        copy.wait_recv()
    tenth()

    for copy in to_owners:
        copy.start()
    for copy in to_owners:
        copy.wait_recv()
    for m in range(NMOM):
        total = mom[tile, m]
        for other in range(ntile - 1):
            total = total + mom_in[other, m]
        out_ref[m] = total * (-1.0 / VECS)
    for group in halos:
        for copy in group:
            copy.wait_send()
    for copy in to_owners:
        copy.wait_send()


def body(ndom, ntile, vectors, positions, onsite, neighbors):
    import functools
    rows = NORB * vectors.shape[1]
    hbm = pl.BlockSpec(memory_space=pltpu.HBM)
    tiles = lambda *lead: pltpu.VMEM((*lead, *TILE), F32)
    result = pl.pallas_call(
        functools.partial(kernel, ndom, ntile),
        out_shape=jax.ShapeDtypeStruct((NMOM, *TILE), F32),
        in_specs=[hbm] * 4,
        out_specs=pl.BlockSpec(memory_space=pltpu.VMEM),
        scratch_shapes=[
            pltpu.VMEM(vectors.shape, F32),
            pltpu.VMEM(positions.shape, F32),
            pltpu.VMEM(onsite.shape, F32),
            pltpu.VMEM(neighbors.shape, jnp.int32),
            tiles(3), tiles(8), pltpu.VMEM((5, *TILE), jnp.int32), pltpu.VMEM((6, *TILE), jnp.int32),
            tiles(7, 8), tiles(4, rows), tiles(4, rows), tiles(4, rows),
            tiles(rows), tiles(rows), tiles(rows), tiles(2 * rows), tiles(2 * rows),
            pltpu.VMEM((2, CODE + 1, LANES), F32),
            pltpu.VMEM((3, 2, 2 * rows, LANES), F32),
            pltpu.VMEM((2, CODE + 1, LANES), F32),
            pltpu.VMEM((3, 2, 2 * rows, LANES), F32),
            tiles(NMOM, NMOM), tiles(ntile - 1, NMOM),
            pltpu.SemaphoreType.DMA((4,)),
            pltpu.SemaphoreType.DMA((4, 2)),
            pltpu.SemaphoreType.DMA((4, 2)),
            pltpu.SemaphoreType.DMA((ntile - 1,)),
            pltpu.SemaphoreType.DMA((ntile - 1,)),
        ],
        compiler_params=pltpu.CompilerParams(
            collective_id=0, has_side_effects=True, vmem_limit_bytes=16 * 1024 * 1024
        ),
        cost_estimate=pl.CostEstimate(flops=10_000_000, bytes_accessed=150_000, transcendentals=10_000),
    )(*[pltpu.with_memory_space_constraint(x, pltpu.HBM) for x in (vectors, positions, onsite, neighbors)])
    return result.reshape(NMOM, GROUPS * LANES)


def solution(mesh):
    import functools
    in_specs = (P(None, "tile", "dom"), P(None, "dom"), P(None, "dom"), P(None, "dom"))
    out_specs = P("tile", "dom")
    local = functools.partial(body, mesh.shape["dom"], mesh.shape["tile"])
    return jax.shard_map(local, mesh=mesh, in_specs=in_specs, out_specs=out_specs, check_vma=False)
```
